32 devices in a mesh: dp: 4 (over x, core), space: 8 (over z, y).
Axes of the slice: x: 2, y: 2, z: 4, core: 2. Of those that a mesh axis runs over, the one named last changes fastest.
Arguments:
- features: bfloat16 [4, 96, 72, 2048], P('dp', 'space'), may hold values from -0.14355469 to 0.14355469
- grad_out: bfloat16 [4, 96, 72, 256], P('dp', 'space'), may hold values from -6 to 6
- weight: bfloat16 [18432, 256], replicated, may hold values from -0.125 to 0.125
- alive: int32 [4], P('dp'), may hold values from 0 to 1, as said below
Outputs:
- weight_grad: float32 [18432, 256], P(('dp', 'space'))
- grad_features: bfloat16 [4, 96, 72, 2048], P('dp', 'space')
The draws below stay inside these ranges and needn't reach their ends.
Inputs may be any that keep to these rules, and one draw needn't show every extreme that they name: `alive`: at least one member survives and at least one does not.
All inputs are finite; a program needn't handle non-finite values.
Results may differ from the reference program's by a relative error of at most 0.001.
Values may be sent and summed in bfloat16 or wider, within the bound.
No kernel may reach another device: no remote copies, remote signals or barrier semaphores. Data moves between devices by JAX's collectives and lax.ppermute only.
A program may use at most 320 MiB of HBM per device.

```python
import jax
import jax.numpy as jnp
from jax import lax

INPUT_CHANNELS = 2048
OUTPUT_CHANNELS = 256
KERNEL_DILATION = 18
MAP_COLUMNS = 72
MEMBERS = 4
MEMBER_ROWS = 96
MEMBER_PIXELS = 6912


def draw_alive(key, part):
    key_flags, key_keep, key_drop = jax.random.split(key, 3)
    flags = (jax.random.randint(key_flags, (MEMBERS,), 0, 4) > 0).astype(jnp.int32)
    keeper = jax.random.randint(key_keep, (), 0, MEMBERS)
    dropped = (keeper + 1 + jax.random.randint(key_drop, (), 0, MEMBERS - 1)) % MEMBERS
    positions = jnp.arange(MEMBERS)
    flags = jnp.where(positions == keeper, 1, flags)
    flags = jnp.where(positions == dropped, 0, flags)
    return flags.astype(jnp.int32)


def levels(key, extent, shards, low, top_value):
    loudness, own = 1.0, jax.random.fold_in(key, 6)
    for position, shards_of in shards:
        heights = jnp.exp(jax.random.uniform(jax.random.fold_in(own, position), (shards_of,), jnp.float32, low / len(shards), top_value / len(shards)))
        loudness = loudness * jnp.repeat(heights, extent[position] // shards_of).reshape([-1 if axis == position else 1 for axis in range(len(extent))])
    return loudness


def scatter_about(stream_key, extent, scale, limit, cuts=(), dtype=jnp.bfloat16):
    factor_of = levels(stream_key, extent, cuts, -0.22, 0.18) if cuts else 1.0
    array = jax.random.normal(stream_key, extent, jnp.float32) * scale * factor_of
    return jnp.minimum(jnp.maximum(array, -limit), limit).astype(dtype)


def setup_inputs(seed: int = 0) -> dict:
    seeds = jax.random.split(jax.random.key(seed), 5)
    features = scatter_about(seeds[0], (MEMBERS, MEMBER_ROWS, MAP_COLUMNS, INPUT_CHANNELS), (2.0 / MEMBER_PIXELS ** 0.5), 0.14355469, ((0, 4), (1, 8)))
    grad_out = scatter_about(seeds[1], (MEMBERS, MEMBER_ROWS, MAP_COLUMNS, OUTPUT_CHANNELS), 1.0, 6.0, ((0, 4), (1, 8)))
    weight = scatter_about(seeds[2], (INPUT_CHANNELS * 9, OUTPUT_CHANNELS), (9 * OUTPUT_CHANNELS) ** -0.5, 0.125)
    alive = draw_alive(jax.random.fold_in(seeds[4], 71), 0)
    return {"features": features, "grad_out": grad_out, "weight": weight, "alive": alive}


def reference(features, grad_out, weight, alive):
    surviving_members = jnp.sum(alive).astype(jnp.float32)
    member_weighting = alive.astype(jnp.float32) / surviving_members
    tap_weights = weight.reshape(INPUT_CHANNELS, 9, OUTPUT_CHANNELS)
    padding_widths = ((KERNEL_DILATION, KERNEL_DILATION), (KERNEL_DILATION, KERNEL_DILATION), (0, 0))

    def member_step(carry, inputs):
        member_image, upstream, scale_now = inputs
        image_padded = jnp.pad(member_image, padding_widths)
        gradient_padded = jnp.pad(upstream, padding_widths)
        flat_grad = upstream.reshape(MEMBER_PIXELS, OUTPUT_CHANNELS)
        columns = []
        input_grad = jnp.zeros((MEMBER_PIXELS, INPUT_CHANNELS), jnp.float32)
        for tap_index in range(9):
            kernel_tap_row = tap_index // 3
            kernel_tap_column = tap_index % 3
            window_slice = image_padded[kernel_tap_row * KERNEL_DILATION:kernel_tap_row * KERNEL_DILATION + MEMBER_ROWS, kernel_tap_column * KERNEL_DILATION:kernel_tap_column * KERNEL_DILATION + MAP_COLUMNS].reshape(MEMBER_PIXELS, INPUT_CHANNELS)
            columns.append(jnp.dot(window_slice.T, flat_grad, preferred_element_type=jnp.float32))
            shifted_rows = gradient_padded[(2 - kernel_tap_row) * KERNEL_DILATION:(2 - kernel_tap_row) * KERNEL_DILATION + MEMBER_ROWS, (2 - kernel_tap_column) * KERNEL_DILATION:(2 - kernel_tap_column) * KERNEL_DILATION + MAP_COLUMNS].reshape(MEMBER_PIXELS, OUTPUT_CHANNELS)
            input_grad = input_grad + jnp.dot(shifted_rows, tap_weights[:, tap_index, :].T, preferred_element_type=jnp.float32)
        kernel_term = jnp.stack(columns, axis=1).reshape(INPUT_CHANNELS * 9, OUTPUT_CHANNELS)
        carry = carry + scale_now * kernel_term
        member_grad = (input_grad * scale_now).astype(jnp.bfloat16).reshape(MEMBER_ROWS, MAP_COLUMNS, INPUT_CHANNELS)
        return carry, member_grad

    start_grad = jnp.zeros((INPUT_CHANNELS * 9, OUTPUT_CHANNELS), jnp.float32)
    weight_grad, grad_features = lax.scan(member_step, start_grad, (features, grad_out, member_weighting))
    return weight_grad, grad_features
```

```python
import functools

import jax
import jax.numpy as jnp
from jax import lax
from jax.experimental import pallas as pl
from jax.experimental.pallas import tpu as pltpu
from jax.sharding import PartitionSpec as P

KERNEL_DILATION = 18
CHANNELS_PER_STEP = 256
F32, F16, BF16 = jnp.float32, jnp.float16, jnp.bfloat16


def from_behind(value, axis, steps):
    count = lax.axis_size(axis)
    leading, last = (max(0, -steps), min(count, count - steps))
    return lax.ppermute(value, axis, [(source, source + steps) for source in range(leading, last)])


def exchange(value, axis, bit):
    return lax.ppermute(value, axis, [(i, i ^ bit) for i in range(lax.axis_size(axis))])


def halo_rows(tile):
    rows = tile.shape[0]
    away, rest = divmod(KERNEL_DILATION, rows)
    below = [from_behind(tile[rest:], "space", -away)]
    above = [from_behind(tile[: rows - rest], "space", away)]
    if rest:
        below.append(from_behind(tile[:rest], "space", -away - 1))
        above.insert(0, from_behind(tile[rows - rest :], "space", away + 1))
    return jnp.concatenate(below), jnp.concatenate(above)


def shift_kernel(columns, *refs):
    out_ref = refs[-1]
    for j, ref in enumerate(refs[:-1]):
        value = ref[...].astype(F32)
        pixels, width = value.shape
        place = lax.broadcasted_iota(jnp.int32, (pixels, width), 0).astype(F32)
        column = place - jnp.floor((place + 0.5) * (1.0 / columns)) * columns
        ahead = pltpu.roll(value, pixels - KERNEL_DILATION, 0)
        behind = pltpu.roll(value, KERNEL_DILATION, 0)
        ahead = jnp.where(column < columns - KERNEL_DILATION, ahead, 0.0)
        behind = jnp.where(column >= KERNEL_DILATION, behind, 0.0)
        base = 3 * j * width
        out_ref[:, base : base + width] = ahead.astype(BF16)
        out_ref[:, base + width : base + 2 * width] = ref[...]
        out_ref[:, base + 2 * width : base + 3 * width] = behind.astype(BF16)


def column_taps(columns, *maps):
    pixels, width = maps[0].shape
    return pl.pallas_call(
        functools.partial(shift_kernel, columns),
        out_shape=jax.ShapeDtypeStruct((pixels, 3 * len(maps) * width), BF16),
        compiler_params=pltpu.CompilerParams(vmem_limit_bytes=40 << 20),
        cost_estimate=pl.CostEstimate(
            flops=0, bytes_accessed=8 * len(maps) * pixels * width, transcendentals=0
        ),
        name="column_taps",
    )(*maps)


def input_grad_kernel(scale_ref, middle_ref, outer_ref, weight_ref, out_ref, wide_ref, taps_ref):
    step = out_ref.shape[1]
    width = weight_ref.shape[1]
    halves = width // 128
    for h in range(halves):
        wide_ref[h] = weight_ref[:, h * 128 : (h + 1) * 128].astype(F32)
    for t in range(9):
        for h in range(halves):
            base = t * width + h * 128
            taps_ref[:, base : base + 128] = wide_ref[h, pl.ds(t, step, stride=9), :].astype(BF16)
    third = 3 * width

    def product(shifted, taps):
        return lax.dot_general(shifted, taps, (((1,), (1,)), ((), ())), preferred_element_type=F32)

    total = product(outer_ref[:, :third], taps_ref[:, :third])
    total += product(middle_ref[...], taps_ref[:, third : 2 * third])
    total += product(outer_ref[:, third:], taps_ref[:, 2 * third :])
    out_ref[...] = (total * scale_ref[0]).astype(BF16)


def input_grad(scale, middle, outer, weight):
    pixels = middle.shape[0]
    rows, width = weight.shape
    channels = rows // 9
    step = CHANNELS_PER_STEP
    return pl.pallas_call(
        input_grad_kernel,
        grid=(channels // step,),
        in_specs=[
            pl.BlockSpec(memory_space=pltpu.SMEM),
            pl.BlockSpec(middle.shape, lambda i: (0, 0)),
            pl.BlockSpec(outer.shape, lambda i: (0, 0)),
            pl.BlockSpec((9 * step, width), lambda i: (i, 0)),
        ],
        out_specs=pl.BlockSpec((pixels, step), lambda i: (0, i)),
        out_shape=jax.ShapeDtypeStruct((pixels, channels), BF16),
        scratch_shapes=[
            pltpu.VMEM((width // 128, 9 * step, 128), F32),
            pltpu.VMEM((step, 9 * width), BF16),
        ],
        compiler_params=pltpu.CompilerParams(vmem_limit_bytes=48 << 20),
        cost_estimate=pl.CostEstimate(
            flops=2 * pixels * rows * width,
            bytes_accessed=2 * (rows * width + pixels * channels + 9 * pixels * width),
            transcendentals=0,
        ),
        name="input_grad",
    )(scale, middle, outer, weight)


def bits_of(axis):
    return [(axis, 1 << k) for k in reversed(range(lax.axis_size(axis).bit_length() - 1))]


def my_bit(axis, bit):
    return (lax.axis_index(axis) // bit) % 2


def pick(value, position, index):
    return lax.dynamic_index_in_dim(value, index, position, keepdims=False)


def scatter_sum(part, names, order):
    names = list(names)
    for name in order:
        position = names.index(name)
        mine = my_bit(*name)
        sent = exchange(pick(part, position, 1 - mine).astype(F16), *name)
        part = pick(part, position, mine).astype(F32) + sent.astype(F32)
        names.pop(position)
    return part


def shards(features, grad_out, weight, alive):
    _, rows, columns, in_channels = features.shape
    out_channels = grad_out.shape[-1]
    pixels = rows * columns
    member_count = lax.axis_size("dp")
    names = bits_of("dp") + bits_of("space")
    core = ("dp", 1)
    others = [name for name in names if name != core]
    dp_high = [name for name in others if name[0] == "dp"]
    space_low = [name for name in others if name[0] == "space"][::-1]

    own_alive = jnp.sum(alive).astype(F32)
    tile = grad_out.reshape(rows, columns, out_channels)
    below, above = halo_rows(tile)
    survivors = own_alive.reshape(1)
    for name in bits_of("dp"):
        survivors = survivors + exchange(survivors, *name)

    term_scale = own_alive * (4.0 / member_count)
    middle = column_taps(columns, tile.reshape(pixels, out_channels))
    outer = column_taps(
        columns, below.reshape(pixels, out_channels), above.reshape(pixels, out_channels)
    )

    cut = features.reshape(pixels, member_count // 2, 2, in_channels // member_count)
    mine = my_bit(*core)
    kept = pick(cut, 2, mine).reshape(pixels, in_channels // 2)
    given = pick(cut, 2, 1 - mine).reshape(pixels, in_channels // 2)

    def term(image, shifted):
        product = lax.dot_general(
            image, shifted, (((0,), (0,)), ((), ())), preferred_element_type=F32
        )
        return product * term_scale

    def pair_sum(shifted):
        sent = exchange(term(given, shifted).astype(F16), *core)
        total = term(kept, shifted) + sent.astype(F32)
        return total.reshape((2,) * len(others) + (-1, shifted.shape[1]))

    y_first = space_low[:1] + space_low[1:] + dp_high
    z_first = space_low[1:] + dp_high + space_low[:1]
    x_first = dp_high + space_low
    width = out_channels
    centre = scatter_sum(pair_sum(middle), others, x_first)
    ring = pair_sum(outer)
    upper = scatter_sum(ring[..., : 3 * width], others, x_first)
    lower = scatter_sum(ring[..., 3 * width : 5 * width], others, y_first)
    last = scatter_sum(ring[..., 5 * width :], others, z_first)
    final = jnp.concatenate([upper, centre, lower, last], axis=1)
    final = final * (member_count * 0.25 / survivors)
    weight_grad = final.reshape(-1, out_channels)

    grad_features = input_grad(own_alive / survivors, middle, outer, weight).reshape(features.shape)
    return (weight_grad, grad_features)


def solution(mesh):
    in_specs = (P("dp", "space", None, None), P("dp", "space", None, None), P(), P("dp"))
    out_specs = (P(("dp", "space"), None), P("dp", "space", None, None))
    return jax.shard_map(shards, mesh=mesh, in_specs=in_specs, out_specs=out_specs, check_vma=False)
```

```python
import functools

import jax
import jax.numpy as jnp
from jax import lax
from jax.experimental import pallas as pl
from jax.experimental.pallas import tpu as pltpu
from jax.sharding import PartitionSpec as P

KERNEL_DILATION = 18
CHANNELS_PER_STEP = 256
F32, F16, BF16 = jnp.float32, jnp.float16, jnp.bfloat16


def from_behind(value, axis, steps):
    count = lax.axis_size(axis)
    leading, last = (max(0, -steps), min(count, count - steps))
    return lax.ppermute(value, axis, [(source, source + steps) for source in range(leading, last)])


def exchange(value, axis, bit):
    return lax.ppermute(value, axis, [(i, i ^ bit) for i in range(lax.axis_size(axis))])


def near_rows(tile):
    away, rest = divmod(KERNEL_DILATION, tile.shape[0])
    below = from_behind(tile[rest:], "space", -away)
    above = from_behind(tile[: tile.shape[0] - rest], "space", away)
    return below, above


def far_rows(tile):
    away, rest = divmod(KERNEL_DILATION, tile.shape[0])
    below = from_behind(tile[:rest], "space", -away - 1)
    above = from_behind(tile[tile.shape[0] - rest :], "space", away + 1)
    return below, above


def flat(piece):
    return piece.reshape(-1, piece.shape[-1])


def shift_columns(columns, pieces, out_ref, base):
    value = jnp.concatenate([ref[...].astype(F32) for ref in pieces])
    pixels, width = value.shape
    place = lax.broadcasted_iota(jnp.int32, (pixels, width), 0).astype(F32)
    column = place - jnp.floor((place + 0.5) * (1.0 / columns)) * columns
    ahead = pltpu.roll(value, pixels - KERNEL_DILATION, 0)
    behind = pltpu.roll(value, KERNEL_DILATION, 0)
    ahead = jnp.where(column < columns - KERNEL_DILATION, ahead, 0.0)
    behind = jnp.where(column >= KERNEL_DILATION, behind, 0.0)
    out_ref[:, base : base + width] = ahead.astype(BF16)
    out_ref[:, base + width : base + 2 * width] = value.astype(BF16)
    out_ref[:, base + 2 * width : base + 3 * width] = behind.astype(BF16)


def shift_rows(columns, cuts, pieces, out_ref):
    at = 0
    for row, cut in enumerate(cuts):
        width = pieces[at].shape[1]
        shift_columns(columns, pieces[at : at + cut], out_ref, 3 * row * width)
        at += cut


def place_in(order, block):
    spot = 0
    for _, bit in order:
        spot = 2 * spot + (block // bit) % 2
    return spot


def relative_member(step, steps):
    half = steps // 2
    return jnp.where(step < half, 2 * step + 1, 2 * (step - half))


def kernel_term_kernel(columns, cuts, order, place_ref, scale_ref, image_ref, *refs):
    pieces, given_ref, kept_ref, shifted_ref = refs[:-3], *refs[-3:]
    step, steps = pl.program_id(0), pl.num_programs(0)

    @pl.when(step == 0)
    def _():
        shift_rows(columns, cuts, pieces, shifted_ref)

    product = jnp.dot(image_ref[...].T, shifted_ref[...], preferred_element_type=F32)
    product = product * scale_ref[0]

    def store(out_ref):
        _, blocks, channels, _ = out_ref.shape
        for j in range(blocks):
            spot = place_in(order, jnp.bitwise_xor(j, place_ref[1]))
            out_ref[0, spot] = product[j * channels : (j + 1) * channels]

    @pl.when(step < steps // 2)
    def _():
        store(given_ref)

    @pl.when(step >= steps // 2)
    def _():
        store(kept_ref)


def kernel_term(columns, place, scale, image, rows_of, order):
    pixels, channels = image.shape
    members, blocks = lax.axis_size("dp"), lax.axis_size("space")
    step, half = channels // members, members // 2
    pieces = [flat(piece) for row in rows_of for piece in row]
    cuts = tuple(len(row) for row in rows_of)
    width = 3 * len(cuts) * pieces[0].shape[1]
    block = (1, blocks, step // blocks, width)
    return pl.pallas_call(
        functools.partial(kernel_term_kernel, columns, cuts, order),
        grid_spec=pltpu.PrefetchScalarGridSpec(
            num_scalar_prefetch=1,
            grid=(members,),
            in_specs=[
                pl.BlockSpec(memory_space=pltpu.SMEM),
                pl.BlockSpec(
                    (pixels, step),
                    lambda i, place: (0, jnp.bitwise_xor(relative_member(i, members), place[0])),
                ),
                *[pl.BlockSpec(piece.shape, lambda i, place: (0, 0)) for piece in pieces],
            ],
            out_specs=[
                pl.BlockSpec(block, lambda i, place: (jnp.minimum(i, half - 1), 0, 0, 0)),
                pl.BlockSpec(block, lambda i, place: (jnp.maximum(i - half, 0), 0, 0, 0)),
            ],
            scratch_shapes=[pltpu.VMEM((pixels, width), BF16)],
        ),
        out_shape=[jax.ShapeDtypeStruct((half, *block[1:]), F32)] * 2,
        compiler_params=pltpu.CompilerParams(vmem_limit_bytes=14 << 20),
        cost_estimate=pl.CostEstimate(
            flops=2 * pixels * channels * width,
            bytes_accessed=2 * pixels * channels + 4 * channels * width,
            transcendentals=0,
        ),
        name="kernel_term",
    )(place, scale, image, *pieces)


def input_grad_kernel(columns, cuts, scale_ref, *refs):
    pieces, weight_ref, out_ref, wide_ref, taps_ref, shifted_ref = refs[:-5], *refs[-5:]
    step = out_ref.shape[1]
    width = weight_ref.shape[1]
    halves = width // 128

    @pl.when(pl.program_id(0) == 0)
    def _():
        shift_rows(columns, cuts, pieces, shifted_ref)

    for h in range(halves):
        wide_ref[h] = weight_ref[:, h * 128 : (h + 1) * 128].astype(F32)
    for t in range(9):
        for h in range(halves):
            base = t * width + h * 128
            taps_ref[:, base : base + 128] = wide_ref[h, pl.ds(t, step, stride=9), :].astype(BF16)
    total = lax.dot_general(
        shifted_ref[...], taps_ref[...], (((1,), (1,)), ((), ())), preferred_element_type=F32
    )
    out_ref[...] = (total * scale_ref[0]).astype(BF16)


def input_grad(columns, scale, rows_of, weight):
    pieces = [flat(piece) for row in rows_of for piece in row]
    cuts = tuple(len(row) for row in rows_of)
    pixels = sum(piece.shape[0] for piece in pieces) // 3
    rows, width = weight.shape
    channels = rows // 9
    step = CHANNELS_PER_STEP
    return pl.pallas_call(
        functools.partial(input_grad_kernel, columns, cuts),
        grid=(channels // step,),
        in_specs=[
            pl.BlockSpec(memory_space=pltpu.SMEM),
            *[pl.BlockSpec(piece.shape, lambda i: (0, 0)) for piece in pieces],
            pl.BlockSpec((9 * step, width), lambda i: (i, 0)),
        ],
        out_specs=pl.BlockSpec((pixels, step), lambda i: (0, i)),
        out_shape=jax.ShapeDtypeStruct((pixels, channels), BF16),
        scratch_shapes=[
            pltpu.VMEM((width // 128, 9 * step, 128), F32),
            pltpu.VMEM((step, 9 * width), BF16),
            pltpu.VMEM((pixels, 9 * width), BF16),
        ],
        compiler_params=pltpu.CompilerParams(vmem_limit_bytes=18 << 20),
        cost_estimate=pl.CostEstimate(
            flops=2 * pixels * rows * width,
            bytes_accessed=2 * (rows * width + pixels * channels),
            transcendentals=0,
        ),
        name="input_grad",
    )(scale, *pieces, pltpu.with_memory_space_constraint(weight, pltpu.HBM))


def bits_of(axis):
    return [(axis, 1 << k) for k in reversed(range(lax.axis_size(axis).bit_length() - 1))]


def after(value, *others):
    return lax.optimization_barrier((value, others))[0]


def exchange_by_role(value, orders, step):
    members, blocks = lax.axis_size("dp"), lax.axis_size("space")
    pairs = []
    for member in range(members):
        for block in range(blocks):
            axis, bit = orders[member % 2][step]
            target = (member ^ bit, block) if axis == "dp" else (member, block ^ bit)
            pairs.append((member * blocks + block, target[0] * blocks + target[1]))
    return lax.ppermute(value, ("dp", "space"), pairs)


class Sums:
    def __init__(self, value, names, orders):
        self.value, self.names, self.orders = value, [list(names), list(names)], orders
        self.even = lax.axis_index("dp") % 2 == 0

    def part(self, index):
        spots = [names.index(order[0]) for names, order in zip(self.names, self.orders)]
        parts = [lax.index_in_dim(self.value, index, spot, keepdims=False) for spot in spots]
        return parts[0] if spots[0] == spots[1] else jnp.where(self.even, *parts)

    def sent(self):
        return self.part(1).astype(F16)

    def add(self, back):
        self.value = self.part(0) + back.astype(F32)
        self.names = [[n for n in names if n != order[0]] for names, order in zip(self.names, self.orders)]
        self.orders = [order[1:] for order in self.orders]


def shards(features, grad_out, weight, alive):
    _, rows, columns, in_channels = features.shape
    out_channels = grad_out.shape[-1]
    pixels = rows * columns
    member_count = lax.axis_size("dp")
    core = ("dp", 1)
    across = [name for name in bits_of("dp") if name != core]
    along = bits_of("space")[::-1]
    first, inner, final_bit = along[:1], along[1:-1], along[-1:]
    orders = (across + first + inner + final_bit, first + inner + across + final_bit)
    centre_order = inner + across + first + final_bit

    own_alive = jnp.sum(alive).astype(F32)
    term_scale = (own_alive * (4.0 / member_count)).reshape(1)
    tile = grad_out.reshape(rows, columns, out_channels)
    image = features.reshape(pixels, in_channels)
    place = jnp.stack([lax.axis_index("dp"), lax.axis_index("space")]).astype(jnp.int32)

    def term(rows_of):
        return kernel_term(columns, place, term_scale, image, rows_of, along)

    def sums(kept, back, *orders):
        value = kept.astype(F32) + back.astype(F32)
        names = across + along
        return Sums(value.reshape((2,) * len(names) + value.shape[2:]), names, orders)

    near_below, near_above = near_rows(tile)
    far_below, far_above = far_rows(tile)
    centre = term([[tile]])
    survivors = own_alive.reshape(1)
    survivors = survivors + exchange(survivors, *core)
    below, above, centre, survivors = lax.optimization_barrier(
        ((near_below, far_below), (far_above, near_above), centre, survivors)
    )

    sent, kept = (half.astype(F16) for half in centre)
    back = exchange(sent, *core)
    for name in across:
        survivors = survivors + exchange(survivors, *name)
    lower = term([after(below, sent, kept)])
    lower, kept, back, survivors = lax.optimization_barrier((lower, kept, back, survivors))
    centre = sums(kept, back, centre_order, centre_order)
    sent, kept = (half.astype(F16) for half in lower)
    back = exchange(sent, *core)
    upper = term([after(above, sent, kept, centre.value)])
    upper, kept, back = lax.optimization_barrier((upper, kept, back))
    sent = upper[0].astype(F16)
    lower = sums(kept, after(back, sent), *orders)
    upper = sums(upper[1], exchange(sent, *core), *orders)

    width = 3 * out_channels
    grad_features = None
    for step, name in enumerate(centre_order):
        ring_sent = [lower.sent(), upper.sent()]
        centre_sent = centre.sent()
        if step + 1 < len(centre_order):
            ring_sent = jnp.concatenate(ring_sent, axis=-1)
            ring_back = exchange_by_role(ring_sent, orders, step)
            centre_back = exchange(centre_sent, *name)
        else:
            ring_back = exchange(jnp.concatenate([*ring_sent, centre_sent], axis=-1), *name)
            centre_back = ring_back[..., 2 * width :]
        if step == 0:
            grad_features = input_grad(
                columns,
                (own_alive / survivors).reshape(1),
                [below, [tile], after(above, ring_sent, centre_sent)],
                weight,
            )
        ring_back, centre_back, grad_features = lax.optimization_barrier(
            (ring_back, centre_back, grad_features)
        )
        lower.add(ring_back[..., :width])
        upper.add(ring_back[..., width : 2 * width])
        centre.add(centre_back)
    final = jnp.concatenate([lower.value, centre.value, upper.value], axis=-1)
    final = final * (member_count * 0.25 / survivors)
    return (final.reshape(-1, out_channels), grad_features.reshape(features.shape))


def solution(mesh):
    in_specs = (P("dp", "space", None, None), P("dp", "space", None, None), P(), P("dp"))
    out_specs = (P(("dp", "space"), None), P("dp", "space", None, None))
    return jax.shard_map(shards, mesh=mesh, in_specs=in_specs, out_specs=out_specs, check_vma=False)
```

```python
import functools

import jax
import jax.numpy as jnp
from jax import lax
from jax.experimental import pallas as pl
from jax.experimental.pallas import tpu as pltpu
from jax.sharding import PartitionSpec as P

KERNEL_DILATION = 18
CHANNELS_PER_STEP = 256
F32, F16, BF16 = jnp.float32, jnp.float16, jnp.bfloat16


def from_behind(value, axis, steps):
    count = lax.axis_size(axis)
    leading, last = (max(0, -steps), min(count, count - steps))
    return lax.ppermute(value, axis, [(source, source + steps) for source in range(leading, last)])


def exchange(value, axis, bit):
    return lax.ppermute(value, axis, [(i, i ^ bit) for i in range(lax.axis_size(axis))])


def near_rows(tile):
    away, rest = divmod(KERNEL_DILATION, tile.shape[0])
    below = from_behind(tile[rest:], "space", -away)
    above = from_behind(tile[: tile.shape[0] - rest], "space", away)
    return below, above


def far_rows(tile):
    away, rest = divmod(KERNEL_DILATION, tile.shape[0])
    below = from_behind(tile[:rest], "space", -away - 1)
    above = from_behind(tile[tile.shape[0] - rest :], "space", away + 1)
    return below, above


def flat(piece):
    return piece.reshape(-1, piece.shape[-1])


def shift_columns(columns, pieces, out_ref, base):
    value = jnp.concatenate([ref[...].astype(F32) for ref in pieces])
    pixels, width = value.shape
    place = lax.broadcasted_iota(jnp.int32, (pixels, width), 0).astype(F32)
    column = place - jnp.floor((place + 0.5) * (1.0 / columns)) * columns
    ahead = pltpu.roll(value, pixels - KERNEL_DILATION, 0)
    behind = pltpu.roll(value, KERNEL_DILATION, 0)
    ahead = jnp.where(column < columns - KERNEL_DILATION, ahead, 0.0)
    behind = jnp.where(column >= KERNEL_DILATION, behind, 0.0)
    out_ref[:, base : base + width] = ahead.astype(BF16)
    out_ref[:, base + width : base + 2 * width] = value.astype(BF16)
    out_ref[:, base + 2 * width : base + 3 * width] = behind.astype(BF16)


def shift_rows(columns, cuts, pieces, out_ref):
    at = 0
    for row, cut in enumerate(cuts):
        width = pieces[at].shape[1]
        shift_columns(columns, pieces[at : at + cut], out_ref, 3 * row * width)
        at += cut


def place_in(order, member, block):
    spot = 0
    for axis, bit in order:
        spot = 2 * spot + ((member if axis == "dp" else block) // bit) % 2
    return spot


def kernel_term_kernel(columns, cuts, orders, parts, place_ref, scale_ref, *refs):
    images, pieces, outs, shifted_ref = refs[:parts], refs[parts:-3], refs[-3:-1], refs[-1]

    @pl.when(pl.program_id(0) == 0)
    def _():
        shift_rows(columns, cuts, pieces, shifted_ref)

    blocks = lax.axis_size("space")

    def products(side, out_ref):
        channels = out_ref.shape[1]
        for i, image_ref in enumerate(images):
            product = jnp.dot(image_ref[...].T, shifted_ref[...], preferred_element_type=F32)
            product = product * scale_ref[0]
            for j in range(blocks):
                block = jnp.bitwise_xor(j, place_ref[1])
                spots = [place_in(order, 2 * i, block) for order in orders]
                spot = jnp.where(place_ref[0] % 2 == side, spots[1], spots[0])
                out_ref[spot] = product[j * channels : (j + 1) * channels]

    for side, out_ref in enumerate(outs):

        @pl.when(pl.program_id(0) == side)
        def _():
            products(side, out_ref)


def kernel_term(columns, place, scale, image, rows_of, orders):
    pixels, channels = image.shape
    members, blocks = lax.axis_size("dp"), lax.axis_size("space")
    step, half = channels // members, members // 2
    pieces = [flat(piece) for row in rows_of for piece in row]
    cuts = tuple(len(row) for row in rows_of)
    width = 3 * len(cuts) * pieces[0].shape[1]

    def segment(i):
        return pl.BlockSpec(
            (pixels, step), lambda side, place: (0, jnp.bitwise_xor(2 * i + 1 - side, place[0]))
        )

    shape = (half * blocks, step // blocks, width)
    return pl.pallas_call(
        functools.partial(kernel_term_kernel, columns, cuts, orders, half),
        grid_spec=pltpu.PrefetchScalarGridSpec(
            num_scalar_prefetch=1,
            grid=(2,),
            in_specs=[
                pl.BlockSpec(memory_space=pltpu.SMEM),
                *[segment(i) for i in range(half)],
                *[pl.BlockSpec(piece.shape, lambda side, place: (0, 0)) for piece in pieces],
            ],
            out_specs=[pl.BlockSpec(shape, lambda side, place: (0, 0, 0))] * 2,
            scratch_shapes=[pltpu.VMEM((pixels, width), BF16)],
        ),
        out_shape=[jax.ShapeDtypeStruct(shape, F32)] * 2,
        compiler_params=pltpu.CompilerParams(vmem_limit_bytes=26 << 20),
        cost_estimate=pl.CostEstimate(
            flops=2 * pixels * channels * width,
            bytes_accessed=2 * pixels * channels + 4 * channels * width,
            transcendentals=0,
        ),
        name="kernel_term",
    )(place, scale, *[image] * half, *pieces)


def input_grad_kernel(columns, cuts, scale_ref, *refs):
    pieces = refs[: sum(cuts)]
    weight_ref = refs[len(pieces)]
    out_ref, wide_ref, taps_ref, shifted_ref = refs[-4:]
    step = out_ref.shape[1]
    width = weight_ref.shape[1]
    halves = width // 128

    @pl.when(pl.program_id(0) == 0)
    def _():
        shift_rows(columns, cuts, pieces, shifted_ref)

    for h in range(halves):
        wide_ref[h] = weight_ref[:, h * 128 : (h + 1) * 128].astype(F32)
    for t in range(9):
        for h in range(halves):
            base = t * width + h * 128
            taps_ref[:, base : base + 128] = wide_ref[h, pl.ds(t, step, stride=9), :].astype(BF16)
    total = lax.dot_general(
        shifted_ref[...], taps_ref[...], (((1,), (1,)), ((), ())), preferred_element_type=F32
    )
    out_ref[...] = (total * scale_ref[0]).astype(BF16)


def input_grad(columns, scale, rows_of, weight, first, count, before=None):
    pieces = [flat(piece) for row in rows_of for piece in row]
    cuts = tuple(len(row) for row in rows_of)
    pixels = sum(piece.shape[0] for piece in pieces) // 3
    rows, width = weight.shape
    channels = rows // 9
    step = CHANNELS_PER_STEP
    earlier = [] if before is None else [before]
    return pl.pallas_call(
        functools.partial(input_grad_kernel, columns, cuts),
        grid=(count,),
        in_specs=[
            pl.BlockSpec(memory_space=pltpu.SMEM),
            *[pl.BlockSpec(piece.shape, lambda i: (0, 0)) for piece in pieces],
            pl.BlockSpec((9 * step, width), lambda i: (i + first, 0)),
            *[pl.BlockSpec(memory_space=pl.ANY) for _ in earlier],
        ],
        out_specs=pl.BlockSpec((pixels, step), lambda i: (0, i + first)),
        out_shape=jax.ShapeDtypeStruct((pixels, channels), BF16),
        input_output_aliases={len(pieces) + 2: 0} if earlier else {},
        scratch_shapes=[
            pltpu.VMEM((width // 128, 9 * step, 128), F32),
            pltpu.VMEM((step, 9 * width), BF16),
            pltpu.VMEM((pixels, 9 * width), BF16),
        ],
        compiler_params=pltpu.CompilerParams(vmem_limit_bytes=18 << 20),
        cost_estimate=pl.CostEstimate(
            flops=2 * pixels * 9 * width * step * count,
            bytes_accessed=2 * (9 * step * width + pixels * step) * count,
            transcendentals=0,
        ),
        name="input_grad",
    )(scale, *pieces, pltpu.with_memory_space_constraint(weight, pltpu.HBM), *earlier)


def bits_of(axis):
    return [(axis, 1 << k) for k in reversed(range(lax.axis_size(axis).bit_length() - 1))]


def after(value, *others):
    return lax.optimization_barrier((value, others))[0]


def exchange_by_role(value, orders, step):
    members, blocks = lax.axis_size("dp"), lax.axis_size("space")
    pairs = []
    for member in range(members):
        for block in range(blocks):
            axis, bit = orders[member % 2][step]
            target = (member ^ bit, block) if axis == "dp" else (member, block ^ bit)
            pairs.append((member * blocks + block, target[0] * blocks + target[1]))
    return lax.ppermute(value, ("dp", "space"), pairs)


def kept(part):
    return part[: part.shape[0] // 2]


def sent(part):
    return part[part.shape[0] // 2 :].astype(F16)


def add(part, back):
    return part.astype(F32) + back.astype(F32)


def shards(features, grad_out, weight, alive):
    _, rows, columns, in_channels = features.shape
    out_channels = grad_out.shape[-1]
    pixels = rows * columns
    member_count = lax.axis_size("dp")
    core = ("dp", 1)
    across = [name for name in bits_of("dp") if name != core]
    along = bits_of("space")[::-1]
    first, inner, final_bit = along[:1], along[1:-1], along[-1:]
    orders = (across + first + inner + final_bit, first + inner + across + final_bit)
    centre_order = inner + across + first + final_bit

    own_alive = jnp.sum(alive).astype(F32)
    term_scale = (own_alive * (4.0 / member_count)).reshape(1)
    tile = grad_out.reshape(rows, columns, out_channels)
    image = features.reshape(pixels, in_channels)
    place = jnp.stack([lax.axis_index("dp"), lax.axis_index("space")]).astype(jnp.int32)

    def term(rows_of, orders, image=image):
        halves = kernel_term(columns, place, term_scale, image, rows_of, orders)
        return [value.astype(F16) for value in halves]

    def in_hbm(value):
        return pltpu.with_memory_space_constraint(value, pltpu.HBM)

    near_below, near_above = near_rows(tile)
    far_below, far_above = far_rows(tile)
    centre = term([[in_hbm(flat(tile))]], [centre_order] * 2, in_hbm(image))
    below, above, centre = lax.optimization_barrier(
        ((near_below, far_below), (far_above, near_above), centre)
    )

    back = exchange(centre[0], *core)
    lower = term([after(below, centre)], orders)
    lower, back = lax.optimization_barrier((lower, back))
    centre = add(centre[1], back)
    back = exchange(lower[0], *core)
    upper = term([after(above, lower, centre)], orders)
    upper, back = lax.optimization_barrier((upper, back))
    upper_back = exchange(upper[0], *core)
    others = [after(own_alive.reshape(1), upper[0])]
    for away in range(1, member_count):
        others.append(exchange(others[0], "dp", away))
    lower = add(lower[1], back)
    upper_back, others = lax.optimization_barrier((upper_back, others))
    upper = add(upper[1], upper_back)
    survivors = sum(others)
    scale = (own_alive / survivors).reshape(1)

    width = 3 * out_channels
    blocks = in_channels // CHANNELS_PER_STEP
    last = len(centre_order) - 1
    rows_of = [below, [in_hbm(flat(tile))], above]
    grad_features = None
    for step, name in enumerate(centre_order):
        ring_sent = [sent(lower), sent(upper)]
        centre_sent = sent(centre)
        if step < last:
            ring_sent = jnp.concatenate(ring_sent, axis=-1)
            centre_back = exchange(centre_sent, *name)
            ring_back = exchange_by_role(ring_sent, orders, step)
        else:
            ring_back = exchange(jnp.concatenate([*ring_sent, centre_sent], axis=-1), *name)
            centre_back = ring_back[..., 2 * width :]
        if step == 0:
            grad_features = input_grad(
                columns, scale, after(rows_of, ring_sent, centre_sent), weight, 0, blocks
            )
        ring_back, centre_back, grad_features = lax.optimization_barrier(
            (ring_back, centre_back, grad_features)
        )
        lower = add(kept(lower), ring_back[..., :width])
        upper = add(kept(upper), ring_back[..., width : 2 * width])
        centre = add(kept(centre), centre_back)
    final = jnp.concatenate([lower[0], centre[0], upper[0]], axis=-1)
    final = final * (member_count * 0.25 / survivors)
    return (final.reshape(-1, out_channels), grad_features.reshape(features.shape))


def solution(mesh):
    in_specs = (P("dp", "space", None, None), P("dp", "space", None, None), P(), P("dp"))
    out_specs = (P(("dp", "space"), None), P("dp", "space", None, None))
    return jax.shard_map(shards, mesh=mesh, in_specs=in_specs, out_specs=out_specs, check_vma=False)
```

```python
import functools

import jax
import jax.numpy as jnp
from jax import lax
from jax.experimental import pallas as pl
from jax.experimental.pallas import tpu as pltpu
from jax.sharding import PartitionSpec as P

KERNEL_DILATION = 18
CHANNELS_PER_STEP = 256
F32, F16, BF16 = jnp.float32, jnp.float16, jnp.bfloat16


def from_behind(value, axis, steps):
    count = lax.axis_size(axis)
    leading, last = (max(0, -steps), min(count, count - steps))
    return lax.ppermute(value, axis, [(source, source + steps) for source in range(leading, last)])


def exchange(value, axis, bit):
    return lax.ppermute(value, axis, [(i, i ^ bit) for i in range(lax.axis_size(axis))])


def either(first, second):
    return jnp.where(lax.axis_index("dp") % 2 == 0, first, second)


def halo_rows(tile):
    members, blocks = lax.axis_size("dp"), lax.axis_size("space")
    away, rest = divmod(KERNEL_DILATION, tile.shape[0])
    assert tile.shape[0] == 2 * rest

    def fetched(value, distance):
        pairs = []
        for member in range(members):
            for block in range(blocks):
                target = block + distance * (1 if member % 2 else -1)
                if 0 <= target < blocks:
                    pairs.append((member * blocks + block, member * blocks + target))
        return lax.ppermute(value, ("dp", "space"), pairs)

    tiles = (tile, exchange(tile, "dp", 1))
    near = fetched(jnp.stack([either(t[rest:], t[:rest]) for t in tiles]), away)
    far = fetched(jnp.stack([either(t[:rest], t[rest:]) for t in tiles]), away + 1)
    return near, far


def flat(piece):
    return piece.reshape(-1, piece.shape[-1])


def shift_columns(columns, pieces, out_ref, base):
    value = jnp.concatenate([ref[...].astype(F32) for ref in pieces])
    pixels, width = value.shape
    place = lax.broadcasted_iota(jnp.int32, (pixels, 128), 0).astype(F32)
    column = place - jnp.floor((place + 0.5) * (1.0 / columns)) * columns
    column = jnp.concatenate([column] * (width // 128), axis=1)
    ahead = pltpu.roll(value, pixels - KERNEL_DILATION, 0)
    behind = pltpu.roll(value, KERNEL_DILATION, 0)
    ahead = jnp.where(column < columns - KERNEL_DILATION, ahead, 0.0)
    behind = jnp.where(column >= KERNEL_DILATION, behind, 0.0)
    out_ref[:, base : base + width] = ahead.astype(BF16)
    out_ref[:, base + width : base + 2 * width] = value.astype(BF16)
    out_ref[:, base + 2 * width : base + 3 * width] = behind.astype(BF16)


def shift_rows(columns, cuts, pieces, out_ref):
    at = 0
    for row, cut in enumerate(cuts):
        width = pieces[at].shape[1]
        shift_columns(columns, pieces[at : at + cut], out_ref, 3 * row * width)
        at += cut


def place_in(order, member, block):
    spot = 0
    for axis, bit in order:
        spot = 2 * spot + ((member if axis == "dp" else block) // bit) % 2
    return spot


def kernel_term_kernel(columns, cuts, streams, parts, turned, place_ref, scale_ref, *refs):
    count = 1 if turned else parts
    images, pieces, outs, shifted_ref = refs[:count], refs[count:-3], refs[-3:-1], refs[-1]
    if not turned:
        pieces, turned_ref = pieces[:-1], pieces[-1]

    @pl.when(pl.program_id(0) == 0)
    def _():
        shift_rows(columns, cuts, pieces, shifted_ref)

    blocks = lax.axis_size("space")

    def products(side, out_ref):
        channels = out_ref.shape[1]
        for i in range(parts):
            if turned:
                image = images[0][0, i]
            else:
                image = images[i][...].T
                turned_ref[0, i] = image
            product = jnp.dot(image, shifted_ref[...], preferred_element_type=F32)
            product = product * scale_ref[0]
            for j in range(blocks):
                block = jnp.bitwise_xor(j, place_ref[1])
                rows = product[j * channels : (j + 1) * channels]
                at = 0
                for width, orders in streams:
                    spots = [place_in(order, 2 * i, block) for order in orders]
                    spot = jnp.where(place_ref[0] % 2 == side, spots[1], spots[0])
                    out_ref[spot, :, at : at + width] = rows[:, at : at + width]
                    at += width

    for side, out_ref in enumerate(outs):

        @pl.when(pl.program_id(0) == side)
        def _():
            products(side, out_ref)


def kernel_term(columns, place, scale, image, rows_of, streams, turned):
    channels = image.size // image.shape[-1] if turned else image.shape[1]
    pixels = image.shape[-1] if turned else image.shape[0]
    members, blocks = lax.axis_size("dp"), lax.axis_size("space")
    step, half = channels // members, members // 2
    pieces = [flat(piece) for row in rows_of for piece in row]
    cuts = tuple(len(row) for row in rows_of)
    width = 3 * len(cuts) * pieces[0].shape[1]

    def segment(i):
        return pl.BlockSpec(
            (pixels, step), lambda side, place: (0, jnp.bitwise_xor(2 * i + 1 - side, place[0]))
        )

    shapes = [(half * blocks, step // blocks, width)] * 2
    turned_block = pl.BlockSpec((1, half, step, pixels), lambda side, place: (side, 0, 0, 0))
    turned_shape = jax.ShapeDtypeStruct((2, half, step, pixels), BF16)
    return pl.pallas_call(
        functools.partial(kernel_term_kernel, columns, cuts, streams, half, turned),
        grid_spec=pltpu.PrefetchScalarGridSpec(
            num_scalar_prefetch=1,
            grid=(2,),
            in_specs=[
                pl.BlockSpec(memory_space=pltpu.SMEM),
                *([turned_block] if turned else [segment(i) for i in range(half)]),
                *[pl.BlockSpec(piece.shape, lambda side, place: (0, 0)) for piece in pieces],
            ],
            out_specs=([] if turned else [turned_block])
            + [pl.BlockSpec(shape, lambda side, place: (0, 0, 0)) for shape in shapes],
            scratch_shapes=[pltpu.VMEM((pixels, width), BF16)],
        ),
        out_shape=([] if turned else [turned_shape])
        + [jax.ShapeDtypeStruct(shape, F32) for shape in shapes],
        compiler_params=pltpu.CompilerParams(vmem_limit_bytes=26 << 20),
        cost_estimate=pl.CostEstimate(
            flops=2 * pixels * channels * width,
            bytes_accessed=2 * pixels * channels + 4 * channels * width,
            transcendentals=0,
        ),
        name="kernel_term",
    )(place, scale, *[image] * (1 if turned else half), *pieces)


def input_grad_kernel(columns, cuts, scale_ref, *refs):
    pieces = refs[: sum(cuts)]
    weight_ref = refs[len(pieces)]
    out_ref, wide_ref, taps_ref, shifted_ref = refs[-4:]
    step = out_ref.shape[1]
    width = weight_ref.shape[1]
    halves = width // 128

    @pl.when(pl.program_id(0) == 0)
    def _():
        shift_rows(columns, cuts, pieces, shifted_ref)

    for h in range(halves):
        wide_ref[h] = weight_ref[:, h * 128 : (h + 1) * 128].astype(F32)
    for t in range(9):
        for h in range(halves):
            base = t * width + h * 128
            taps_ref[:, base : base + 128] = wide_ref[h, pl.ds(t, step, stride=9), :].astype(BF16)
    total = lax.dot_general(
        shifted_ref[...], taps_ref[...], (((1,), (1,)), ((), ())), preferred_element_type=F32
    )
    out_ref[...] = (total * scale_ref[0]).astype(BF16)


def input_grad(columns, scale, rows_of, weight, first, count, before=None):
    pieces = [flat(piece) for row in rows_of for piece in row]
    cuts = tuple(len(row) for row in rows_of)
    pixels = sum(piece.shape[0] for piece in pieces) // 3
    rows, width = weight.shape
    channels = rows // 9
    step = CHANNELS_PER_STEP
    earlier = [] if before is None else [before]
    return pl.pallas_call(
        functools.partial(input_grad_kernel, columns, cuts),
        grid=(count,),
        in_specs=[
            pl.BlockSpec(memory_space=pltpu.SMEM),
            *[pl.BlockSpec(piece.shape, lambda i: (0, 0)) for piece in pieces],
            pl.BlockSpec((9 * step, width), lambda i: (i + first, 0)),
            *[pl.BlockSpec(memory_space=pl.ANY) for _ in earlier],
        ],
        out_specs=pl.BlockSpec((pixels, step), lambda i: (0, i + first)),
        out_shape=jax.ShapeDtypeStruct((pixels, channels), BF16),
        input_output_aliases={len(pieces) + 2: 0} if earlier else {},
        scratch_shapes=[
            pltpu.VMEM((width // 128, 9 * step, 128), F32),
            pltpu.VMEM((step, 9 * width), BF16),
            pltpu.VMEM((pixels, 9 * width), BF16),
        ],
        compiler_params=pltpu.CompilerParams(vmem_limit_bytes=18 << 20),
        cost_estimate=pl.CostEstimate(
            flops=2 * pixels * 9 * width * step * count,
            bytes_accessed=2 * (9 * step * width + pixels * step) * count,
            transcendentals=0,
        ),
        name="input_grad",
    )(scale, *pieces, pltpu.with_memory_space_constraint(weight, pltpu.HBM), *earlier)


def bits_of(axis):
    return [(axis, 1 << k) for k in reversed(range(lax.axis_size(axis).bit_length() - 1))]


def after(value, *others):
    return lax.optimization_barrier((value, others))[0]


def exchange_by_role(value, orders, step):
    members, blocks = lax.axis_size("dp"), lax.axis_size("space")
    pairs = []
    for member in range(members):
        for block in range(blocks):
            axis, bit = orders[member % 2][step]
            target = (member ^ bit, block) if axis == "dp" else (member, block ^ bit)
            pairs.append((member * blocks + block, target[0] * blocks + target[1]))
    return lax.ppermute(value, ("dp", "space"), pairs)


def kept(part):
    return part[: part.shape[0] // 2]


def sent(part):
    return part[part.shape[0] // 2 :].astype(F16)


def add(part, back):
    return part.astype(F32) + back.astype(F32)


def shards(features, grad_out, weight, alive):
    _, rows, columns, in_channels = features.shape
    out_channels = grad_out.shape[-1]
    pixels = rows * columns
    member_count = lax.axis_size("dp")
    core = ("dp", 1)
    across = [name for name in bits_of("dp") if name != core]
    along = bits_of("space")[::-1]
    first, inner, final_bit = along[:1], along[1:-1], along[-1:]
    orders = (across + first + inner + final_bit, first + inner + across + final_bit)
    centre_order = inner + across + first + final_bit

    own_alive = jnp.sum(alive).astype(F32)
    term_scale = (own_alive * (4.0 / member_count)).reshape(1)
    tile = grad_out.reshape(rows, columns, out_channels)
    image = features.reshape(pixels, in_channels)
    place = jnp.stack([lax.axis_index("dp"), lax.axis_index("space")]).astype(jnp.int32)

    def term(image, rows_of, streams, turned=True):
        *given, first, second = kernel_term(
            columns, place, term_scale, image, rows_of, streams, turned
        )
        return [*given, first.astype(F16), second.astype(F16)]

    def in_hbm(value):
        return pltpu.with_memory_space_constraint(value, pltpu.HBM)

    near, far = halo_rows(tile)
    width = 3 * out_channels
    image, *centre = term(
        in_hbm(image), [[in_hbm(flat(tile))]], [(width, [centre_order] * 2)], False
    )
    alive_all = [own_alive.reshape(1)]
    for away in range(1, member_count):
        alive_all.append(exchange(alive_all[0], "dp", away))
    near, far, centre, alive_all = lax.optimization_barrier((near, far, centre, alive_all))
    survivors = sum(alive_all)
    scale = own_alive / survivors

    first_rows = either(near[0], far[0]), either(far[0], near[0])
    other = exchange(jnp.stack([near[1], far[1]]), *core)
    back = exchange(centre[0], *core)
    first = term(image, [after(first_rows, centre)], [(width, orders)])
    first, other, back = lax.optimization_barrier((first, other, back))
    second_rows = either(other[1], other[0]), either(other[0], other[1])
    centre = add(centre[1], back)
    back = exchange(first[0], *core)
    second = term(image, [after(second_rows, first, centre)], [(width, orders)])
    second, back = lax.optimization_barrier((second, back))
    ring = [None, add(second[1], back)]
    below = [either(*rows) for rows in zip(first_rows, second_rows)]
    above = [either(*rows) for rows in zip(second_rows, first_rows)]
    back, scale, below, above = lax.optimization_barrier(
        (exchange(second[0], *core), scale, below, above)
    )
    ring[0] = add(first[1], back)

    blocks = in_channels // CHANNELS_PER_STEP
    early = blocks * 6 // 8
    last = len(centre_order) - 1
    rows_of = [below, [in_hbm(flat(tile))], above]
    grad_features = None
    for step, name in enumerate(centre_order):
        ring_sent = jnp.concatenate([sent(part) for part in ring], axis=-1)
        ring_back = exchange_by_role(ring_sent, orders, step)
        if step:
            centre = add(kept(centre), after(centre_back, ring_sent))
        centre_sent = sent(centre)
        centre_back = exchange(centre_sent, *name)
        if step in (0, last):
            grad_features = input_grad(
                columns,
                scale,
                after(rows_of, ring_sent, centre_sent),
                weight,
                early if step else 0,
                blocks - early if step else early,
                grad_features,
            )
            ring_back, grad_features = lax.optimization_barrier((ring_back, grad_features))
        ring = [
            add(kept(part), ring_back[..., width * i : width * (i + 1)])
            for i, part in enumerate(ring)
        ]
    centre = add(kept(centre), centre_back)
    first, second = (part[0] for part in ring)
    final = jnp.concatenate([either(first, second), centre[0], either(second, first)], axis=-1)
    final = final * (member_count * 0.25 / survivors)
    return (final.reshape(-1, out_channels), grad_features.reshape(features.shape))


def solution(mesh):
    in_specs = (P("dp", "space", None, None), P("dp", "space", None, None), P(), P("dp"))
    out_specs = (P(("dp", "space"), None), P("dp", "space", None, None))
    return jax.shard_map(shards, mesh=mesh, in_specs=in_specs, out_specs=out_specs, check_vma=False)
```

```python
import functools

import jax
import jax.numpy as jnp
from jax import lax
from jax.experimental import pallas as pl
from jax.experimental.pallas import tpu as pltpu
from jax.sharding import PartitionSpec as P

KERNEL_DILATION = 18
CHANNELS_PER_STEP = 256
F32, F16, BF16 = jnp.float32, jnp.float16, jnp.bfloat16


def from_behind(value, axis, steps):
    count = lax.axis_size(axis)
    leading, last = (max(0, -steps), min(count, count - steps))
    return lax.ppermute(value, axis, [(source, source + steps) for source in range(leading, last)])


def exchange(value, axis, bit):
    return lax.ppermute(value, axis, [(i, i ^ bit) for i in range(lax.axis_size(axis))])


def either(first, second):
    return jnp.where(lax.axis_index("dp") % 2 == 0, first, second)


def halo_rows(tile):
    members, blocks = lax.axis_size("dp"), lax.axis_size("space")
    away, rest = divmod(KERNEL_DILATION, tile.shape[0])
    assert tile.shape[0] == 2 * rest

    def fetched(value, distance):
        pairs = []
        for member in range(members):
            for block in range(blocks):
                target = block + distance * (1 if member % 2 else -1)
                if 0 <= target < blocks:
                    pairs.append((member * blocks + block, member * blocks + target))
        return lax.ppermute(value, ("dp", "space"), pairs)

    tiles = (tile, exchange(tile, "dp", 1))
    near = fetched(jnp.stack([either(t[rest:], t[:rest]) for t in tiles]), away)
    far = fetched(jnp.stack([either(t[:rest], t[rest:]) for t in tiles]), away + 1)
    return near, far


def flat(piece):
    return piece.reshape(-1, piece.shape[-1])


def shift_columns(columns, pieces, out_ref, base):
    value = jnp.concatenate([ref[...].astype(F32) for ref in pieces])
    pixels, width = value.shape
    place = lax.broadcasted_iota(jnp.int32, (pixels, 128), 0).astype(F32)
    column = place - jnp.floor((place + 0.5) * (1.0 / columns)) * columns
    column = jnp.concatenate([column] * (width // 128), axis=1)
    ahead = pltpu.roll(value, pixels - KERNEL_DILATION, 0)
    behind = pltpu.roll(value, KERNEL_DILATION, 0)
    ahead = jnp.where(column < columns - KERNEL_DILATION, ahead, 0.0)
    behind = jnp.where(column >= KERNEL_DILATION, behind, 0.0)
    out_ref[:, base : base + width] = ahead.astype(BF16)
    out_ref[:, base + width : base + 2 * width] = value.astype(BF16)
    out_ref[:, base + 2 * width : base + 3 * width] = behind.astype(BF16)


def shift_rows(columns, cuts, pieces, out_ref):
    at = 0
    for row, cut in enumerate(cuts):
        width = pieces[at].shape[1]
        shift_columns(columns, pieces[at : at + cut], out_ref, 3 * row * width)
        at += cut


def place_in(order, member, block):
    spot = 0
    for axis, bit in order:
        spot = 2 * spot + ((member if axis == "dp" else block) // bit) % 2
    return spot


def kernel_term_kernel(columns, cuts, streams, parts, turned, place_ref, scale_ref, *refs):
    count = 1 if turned else parts
    images, pieces, outs, shifted_ref = refs[:count], refs[count:-3], refs[-3:-1], refs[-1]
    if not turned:
        pieces, turned_ref = pieces[:-1], pieces[-1]

    @pl.when(pl.program_id(0) == 0)
    def _():
        shift_rows(columns, cuts, pieces, shifted_ref)

    blocks = lax.axis_size("space")

    def products(side, out_ref):
        channels = out_ref.shape[1]
        for i in range(parts):
            if turned:
                image = images[0][0, i]
            else:
                image = images[i][...].T
                turned_ref[0, i] = image
            product = jnp.dot(image, shifted_ref[...], preferred_element_type=F32)
            product = product * scale_ref[0]
            for j in range(blocks):
                block = jnp.bitwise_xor(j, place_ref[1])
                rows = product[j * channels : (j + 1) * channels]
                at = 0
                for width, orders in streams:
                    spots = [place_in(order, 2 * i, block) for order in orders]
                    spot = jnp.where(place_ref[0] % 2 == side, spots[1], spots[0])
                    out_ref[spot, :, at : at + width] = rows[:, at : at + width]
                    at += width

    for side, out_ref in enumerate(outs):

        @pl.when(pl.program_id(0) == side)
        def _():
            products(side, out_ref)


def kernel_term(columns, place, scale, image, rows_of, streams, turned):
    channels = image.size // image.shape[-1] if turned else image.shape[1]
    pixels = image.shape[-1] if turned else image.shape[0]
    members, blocks = lax.axis_size("dp"), lax.axis_size("space")
    step, half = channels // members, members // 2
    pieces = [flat(piece) for row in rows_of for piece in row]
    cuts = tuple(len(row) for row in rows_of)
    width = 3 * len(cuts) * pieces[0].shape[1]

    def segment(i):
        return pl.BlockSpec(
            (pixels, step), lambda side, place: (0, jnp.bitwise_xor(2 * i + 1 - side, place[0]))
        )

    shapes = [(half * blocks, step // blocks, width)] * 2
    turned_block = pl.BlockSpec((1, half, step, pixels), lambda side, place: (side, 0, 0, 0))
    turned_shape = jax.ShapeDtypeStruct((2, half, step, pixels), BF16)
    return pl.pallas_call(
        functools.partial(kernel_term_kernel, columns, cuts, streams, half, turned),
        grid_spec=pltpu.PrefetchScalarGridSpec(
            num_scalar_prefetch=1,
            grid=(2,),
            in_specs=[
                pl.BlockSpec(memory_space=pltpu.SMEM),
                *([turned_block] if turned else [segment(i) for i in range(half)]),
                *[pl.BlockSpec(piece.shape, lambda side, place: (0, 0)) for piece in pieces],
            ],
            out_specs=([] if turned else [turned_block])
            + [pl.BlockSpec(shape, lambda side, place: (0, 0, 0)) for shape in shapes],
            scratch_shapes=[pltpu.VMEM((pixels, width), BF16)],
        ),
        out_shape=([] if turned else [turned_shape])
        + [jax.ShapeDtypeStruct(shape, F32) for shape in shapes],
        compiler_params=pltpu.CompilerParams(vmem_limit_bytes=26 << 20),
        cost_estimate=pl.CostEstimate(
            flops=2 * pixels * channels * width,
            bytes_accessed=2 * pixels * channels + 4 * channels * width,
            transcendentals=0,
        ),
        name="kernel_term",
    )(place, scale, *[image] * (1 if turned else half), *pieces)


def input_grad_kernel(columns, cuts, scale_ref, *refs):
    pieces = refs[: sum(cuts)]
    weight_ref = refs[len(pieces)]
    out_ref, wide_ref, taps_ref, shifted_ref = refs[-4:]
    step = out_ref.shape[1]
    width = weight_ref.shape[1]
    halves = width // 128

    @pl.when(pl.program_id(0) == 0)
    def _():
        shift_rows(columns, cuts, pieces, shifted_ref)

    for h in range(halves):
        wide_ref[h] = weight_ref[:, h * 128 : (h + 1) * 128].astype(F32)
    for t in range(9):
        for h in range(halves):
            base = t * width + h * 128
            taps_ref[:, base : base + 128] = wide_ref[h, pl.ds(t, step, stride=9), :].astype(BF16)
    total = lax.dot_general(
        shifted_ref[...], taps_ref[...], (((1,), (1,)), ((), ())), preferred_element_type=F32
    )
    out_ref[...] = (total * scale_ref[0]).astype(BF16)


def input_grad(columns, scale, rows_of, weight, first, count, before=None):
    pieces = [flat(piece) for row in rows_of for piece in row]
    cuts = tuple(len(row) for row in rows_of)
    pixels = sum(piece.shape[0] for piece in pieces) // 3
    rows, width = weight.shape
    channels = rows // 9
    step = CHANNELS_PER_STEP
    earlier = [] if before is None else [before]
    return pl.pallas_call(
        functools.partial(input_grad_kernel, columns, cuts),
        grid=(count,),
        in_specs=[
            pl.BlockSpec(memory_space=pltpu.SMEM),
            *[pl.BlockSpec(piece.shape, lambda i: (0, 0)) for piece in pieces],
            pl.BlockSpec((9 * step, width), lambda i: (i + first, 0)),
            *[pl.BlockSpec(memory_space=pl.ANY) for _ in earlier],
        ],
        out_specs=pl.BlockSpec((pixels, step), lambda i: (0, i + first)),
        out_shape=jax.ShapeDtypeStruct((pixels, channels), BF16),
        input_output_aliases={len(pieces) + 2: 0} if earlier else {},
        scratch_shapes=[
            pltpu.VMEM((width // 128, 9 * step, 128), F32),
            pltpu.VMEM((step, 9 * width), BF16),
            pltpu.VMEM((pixels, 9 * width), BF16),
        ],
        compiler_params=pltpu.CompilerParams(vmem_limit_bytes=18 << 20),
        cost_estimate=pl.CostEstimate(
            flops=2 * pixels * 9 * width * step * count,
            bytes_accessed=2 * (9 * step * width + pixels * step) * count,
            transcendentals=0,
        ),
        name="input_grad",
    )(scale, *pieces, pltpu.with_memory_space_constraint(weight, pltpu.HBM), *earlier)


def bits_of(axis):
    return [(axis, 1 << k) for k in reversed(range(lax.axis_size(axis).bit_length() - 1))]


def after(value, *others):
    return lax.optimization_barrier((value, others))[0]


def exchange_by_role(value, orders, step):
    members, blocks = lax.axis_size("dp"), lax.axis_size("space")
    pairs = []
    for member in range(members):
        for block in range(blocks):
            axis, bit = orders[member % 2][step]
            target = (member ^ bit, block) if axis == "dp" else (member, block ^ bit)
            pairs.append((member * blocks + block, target[0] * blocks + target[1]))
    return lax.ppermute(value, ("dp", "space"), pairs)


def kept(part):
    return part[: part.shape[0] // 2]


def sent(part):
    return part[part.shape[0] // 2 :].astype(F16)


def add(part, back):
    return part.astype(F32) + back.astype(F32)


def shards(features, grad_out, weight, alive):
    _, rows, columns, in_channels = features.shape
    out_channels = grad_out.shape[-1]
    pixels = rows * columns
    member_count = lax.axis_size("dp")
    core = ("dp", 1)
    across = [name for name in bits_of("dp") if name != core]
    along = bits_of("space")[::-1]
    first, inner, final_bit = along[:1], along[1:-1], along[-1:]
    orders = (across + first + inner + final_bit, first + inner + across + final_bit)
    centre_order = inner + across + first + final_bit

    own_alive = jnp.sum(alive).astype(F32)
    term_scale = (own_alive * (4.0 / member_count)).reshape(1)
    tile = grad_out.reshape(rows, columns, out_channels)
    image = features.reshape(pixels, in_channels)
    place = jnp.stack([lax.axis_index("dp"), lax.axis_index("space")]).astype(jnp.int32)

    def term(image, rows_of, streams, turned=True):
        *given, first, second = kernel_term(
            columns, place, term_scale, image, rows_of, streams, turned
        )
        return [*given, first.astype(F16), second.astype(F16)]

    def in_hbm(value):
        return pltpu.with_memory_space_constraint(value, pltpu.HBM)

    near, far = halo_rows(tile)
    width = 3 * out_channels
    image, *centre = term(
        in_hbm(image), [[in_hbm(flat(tile))]], [(width, [centre_order] * 2)], False
    )
    alive_all = [own_alive.reshape(1)]
    for away in range(1, member_count):
        alive_all.append(exchange(alive_all[0], "dp", away))
    near, far, centre, alive_all = lax.optimization_barrier((near, far, centre, alive_all))

    first_rows = either(near[0], far[0]), either(far[0], near[0])
    other = exchange(jnp.stack([near[1], far[1]]), *core)
    back = exchange(centre[0], *core)
    first = term(image, [after(first_rows, centre)], [(width, orders)])
    first, other, back = lax.optimization_barrier((first, other, back))
    second_rows = either(other[1], other[0]), either(other[0], other[1])
    centre = add(centre[1], back)
    back = exchange(first[0], *core)
    second = term(image, [after(second_rows, first, centre)], [(width, orders)])
    second, back = lax.optimization_barrier((second, back))
    ring = [None, add(second[1], back)]
    below = [either(*rows) for rows in zip(first_rows, second_rows)]
    above = [either(*rows) for rows in zip(second_rows, first_rows)]
    back, below, above = lax.optimization_barrier((exchange(second[0], *core), below, above))
    ring[0] = add(first[1], back)

    blocks = in_channels // CHANNELS_PER_STEP
    early = blocks * 4 // 8
    last = len(centre_order) - 1
    rows_of = [below, [in_hbm(flat(tile))], above]
    chains = [[ring[1], orders, None], [centre, (centre_order, centre_order), None], [ring[0], orders, None]]
    grad_features = token = None
    for step in range(last):
        operands = []
        for chain in chains if step == 0 else [chains[i] for i in (0,1,2)]:
            part, order, back = chain
            if step:
                part = add(kept(part), after(back, token))
            token = sent(part)
            operands.append(token)
            chain[0], chain[2] = part, exchange_by_role(token, order, step)
        if step == 0:
            survivors = sum(after(alive_all, *operands))
            scale = own_alive / survivors
            grad_features = input_grad(
                columns, scale, after(rows_of, *operands), weight, 0, early, grad_features
            )
            token = grad_features
    parts = []
    for part, order, back in chains:
        parts.append(add(kept(part), after(back, token)))
        token = sent(parts[-1])
    operands = jnp.concatenate([sent(part) for part in parts], axis=-1)
    back = exchange(operands, *centre_order[last])
    grad_features = input_grad(
        columns, scale, after(rows_of, operands), weight, early, blocks - early, grad_features
    )
    back, grad_features = lax.optimization_barrier((back, grad_features))
    parts = [add(kept(part), back[..., width * i : width * (i + 1)]) for i, part in enumerate(parts)]
    second, centre, first = (part[0] for part in parts)
    final = jnp.concatenate([either(first, second), centre, either(second, first)], axis=-1)
    final = final * (member_count * 0.25 / survivors)
    return (final.reshape(-1, out_channels), grad_features.reshape(features.shape))


def solution(mesh):
    in_specs = (P("dp", "space", None, None), P("dp", "space", None, None), P(), P("dp"))
    out_specs = (P(("dp", "space"), None), P("dp", "space", None, None))
    return jax.shard_map(shards, mesh=mesh, in_specs=in_specs, out_specs=out_specs, check_vma=False)
```

```python
import functools

import jax
import jax.numpy as jnp
from jax import lax
from jax.experimental import pallas as pl
from jax.experimental.pallas import tpu as pltpu
from jax.sharding import PartitionSpec as P

KERNEL_DILATION = 18
CHANNELS_PER_STEP = 256
F32, F16, BF16 = jnp.float32, jnp.float16, jnp.bfloat16


def from_behind(value, axis, steps):
    count = lax.axis_size(axis)
    leading, last = (max(0, -steps), min(count, count - steps))
    return lax.ppermute(value, axis, [(source, source + steps) for source in range(leading, last)])


def exchange(value, axis, bit):
    return lax.ppermute(value, axis, [(i, i ^ bit) for i in range(lax.axis_size(axis))])


def either(first, second):
    return jnp.where(lax.axis_index("dp") % 2 == 0, first, second)


def halo_rows(tile):
    members, blocks = lax.axis_size("dp"), lax.axis_size("space")
    away, rest = divmod(KERNEL_DILATION, tile.shape[0])
    assert tile.shape[0] == 2 * rest

    def fetched(value, distance):
        pairs = []
        for member in range(members):
            for block in range(blocks):
                target = block + distance * (1 if member % 2 else -1)
                if 0 <= target < blocks:
                    pairs.append((member * blocks + block, member * blocks + target))
        return lax.ppermute(value, ("dp", "space"), pairs)

    tiles = (tile, exchange(tile, "dp", 1))
    near = fetched(jnp.stack([either(t[rest:], t[:rest]) for t in tiles]), away)
    far = fetched(jnp.stack([either(t[:rest], t[rest:]) for t in tiles]), away + 1)
    return near, far


def flat(piece):
    return piece.reshape(-1, piece.shape[-1])


def shift_columns(columns, pieces, out_ref, base):
    value = jnp.concatenate([ref[...].astype(F32) for ref in pieces])
    pixels, width = value.shape
    place = lax.broadcasted_iota(jnp.int32, (pixels, 128), 0).astype(F32)
    column = place - jnp.floor((place + 0.5) * (1.0 / columns)) * columns
    column = jnp.concatenate([column] * (width // 128), axis=1)
    ahead = pltpu.roll(value, pixels - KERNEL_DILATION, 0)
    behind = pltpu.roll(value, KERNEL_DILATION, 0)
    ahead = jnp.where(column < columns - KERNEL_DILATION, ahead, 0.0)
    behind = jnp.where(column >= KERNEL_DILATION, behind, 0.0)
    out_ref[:, base : base + width] = ahead.astype(BF16)
    out_ref[:, base + width : base + 2 * width] = value.astype(BF16)
    out_ref[:, base + 2 * width : base + 3 * width] = behind.astype(BF16)


def shift_rows(columns, cuts, pieces, out_ref):
    at = 0
    for row, cut in enumerate(cuts):
        width = pieces[at].shape[1]
        shift_columns(columns, pieces[at : at + cut], out_ref, 3 * row * width)
        at += cut


def place_in(order, member, block):
    spot = 0
    for axis, bit in order:
        spot = 2 * spot + ((member if axis == "dp" else block) // bit) % 2
    return spot


def kernel_term_kernel(columns, cuts, streams, parts, turned, place_ref, scale_ref, *refs):
    count = 1 if turned else parts
    images, pieces, outs, shifted_ref = refs[:count], refs[count:-3], refs[-3:-1], refs[-1]
    if not turned:
        pieces, turned_ref = pieces[:-1], pieces[-1]

    @pl.when(pl.program_id(0) == 0)
    def _():
        shift_rows(columns, cuts, pieces, shifted_ref)

    blocks = lax.axis_size("space")

    def products(side, out_ref):
        channels = out_ref.shape[1]
        for i in range(parts):
            if turned:
                image = images[0][0, i]
            else:
                image = images[i][...].T
                turned_ref[0, i] = image
            product = jnp.dot(image, shifted_ref[...], preferred_element_type=F32)
            product = product * scale_ref[0]
            for j in range(blocks):
                block = jnp.bitwise_xor(j, place_ref[1])
                rows = product[j * channels : (j + 1) * channels]
                at = 0
                for width, orders in streams:
                    spots = [place_in(order, 2 * i, block) for order in orders]
                    spot = jnp.where(place_ref[0] % 2 == side, spots[1], spots[0])
                    out_ref[spot, :, at : at + width] = rows[:, at : at + width]
                    at += width

    for side, out_ref in enumerate(outs):

        @pl.when(pl.program_id(0) == side)
        def _():
            products(side, out_ref)


def kernel_term(columns, place, scale, image, rows_of, streams, turned):
    channels = image.size // image.shape[-1] if turned else image.shape[1]
    pixels = image.shape[-1] if turned else image.shape[0]
    members, blocks = lax.axis_size("dp"), lax.axis_size("space")
    step, half = channels // members, members // 2
    pieces = [flat(piece) for row in rows_of for piece in row]
    cuts = tuple(len(row) for row in rows_of)
    width = 3 * len(cuts) * pieces[0].shape[1]

    def segment(i):
        return pl.BlockSpec(
            (pixels, step), lambda side, place: (0, jnp.bitwise_xor(2 * i + 1 - side, place[0]))
        )

    shapes = [(half * blocks, step // blocks, width)] * 2
    turned_block = pl.BlockSpec((1, half, step, pixels), lambda side, place: (side, 0, 0, 0))
    turned_shape = jax.ShapeDtypeStruct((2, half, step, pixels), BF16)
    return pl.pallas_call(
        functools.partial(kernel_term_kernel, columns, cuts, streams, half, turned),
        grid_spec=pltpu.PrefetchScalarGridSpec(
            num_scalar_prefetch=1,
            grid=(2,),
            in_specs=[
                pl.BlockSpec(memory_space=pltpu.SMEM),
                *([turned_block] if turned else [segment(i) for i in range(half)]),
                *[pl.BlockSpec(piece.shape, lambda side, place: (0, 0)) for piece in pieces],
            ],
            out_specs=([] if turned else [turned_block])
            + [pl.BlockSpec(shape, lambda side, place: (0, 0, 0)) for shape in shapes],
            scratch_shapes=[pltpu.VMEM((pixels, width), BF16)],
        ),
        out_shape=([] if turned else [turned_shape])
        + [jax.ShapeDtypeStruct(shape, F32) for shape in shapes],
        compiler_params=pltpu.CompilerParams(vmem_limit_bytes=26 << 20),
        cost_estimate=pl.CostEstimate(
            flops=2 * pixels * channels * width,
            bytes_accessed=2 * pixels * channels + 4 * channels * width,
            transcendentals=0,
        ),
        name="kernel_term",
    )(place, scale, *[image] * (1 if turned else half), *pieces)


def input_grad_kernel(columns, cuts, scale_ref, *refs):
    pieces = refs[: sum(cuts)]
    weight_ref = refs[len(pieces)]
    out_ref, wide_ref, taps_ref, shifted_ref = refs[-4:]
    step = out_ref.shape[1]
    width = weight_ref.shape[1]
    halves = width // 128

    @pl.when(pl.program_id(0) == 0)
    def _():
        shift_rows(columns, cuts, pieces, shifted_ref)

    for h in range(halves):
        wide_ref[h] = weight_ref[:, h * 128 : (h + 1) * 128].astype(F32)
    for t in range(9):
        for h in range(halves):
            base = t * width + h * 128
            taps_ref[:, base : base + 128] = wide_ref[h, pl.ds(t, step, stride=9), :].astype(BF16)
    total = lax.dot_general(
        shifted_ref[...], taps_ref[...], (((1,), (1,)), ((), ())), preferred_element_type=F32
    )
    out_ref[...] = (total * scale_ref[0]).astype(BF16)


def input_grad(columns, scale, rows_of, weight, first, count, before=None):
    pieces = [flat(piece) for row in rows_of for piece in row]
    cuts = tuple(len(row) for row in rows_of)
    pixels = sum(piece.shape[0] for piece in pieces) // 3
    rows, width = weight.shape
    channels = rows // 9
    step = CHANNELS_PER_STEP
    earlier = [] if before is None else [before]
    return pl.pallas_call(
        functools.partial(input_grad_kernel, columns, cuts),
        grid=(count,),
        in_specs=[
            pl.BlockSpec(memory_space=pltpu.SMEM),
            *[pl.BlockSpec(piece.shape, lambda i: (0, 0)) for piece in pieces],
            pl.BlockSpec((9 * step, width), lambda i: (i + first, 0)),
            *[pl.BlockSpec(memory_space=pl.ANY) for _ in earlier],
        ],
        out_specs=pl.BlockSpec((pixels, step), lambda i: (0, i + first)),
        out_shape=jax.ShapeDtypeStruct((pixels, channels), BF16),
        input_output_aliases={len(pieces) + 2: 0} if earlier else {},
        scratch_shapes=[
            pltpu.VMEM((width // 128, 9 * step, 128), F32),
            pltpu.VMEM((step, 9 * width), BF16),
            pltpu.VMEM((pixels, 9 * width), BF16),
        ],
        compiler_params=pltpu.CompilerParams(vmem_limit_bytes=18 << 20),
        cost_estimate=pl.CostEstimate(
            flops=2 * pixels * 9 * width * step * count,
            bytes_accessed=2 * (9 * step * width + pixels * step) * count,
            transcendentals=0,
        ),
        name="input_grad",
    )(scale, *pieces, pltpu.with_memory_space_constraint(weight, pltpu.HBM), *earlier)


def bits_of(axis):
    return [(axis, 1 << k) for k in reversed(range(lax.axis_size(axis).bit_length() - 1))]


def after(value, *others):
    return lax.optimization_barrier((value, others))[0]


def exchange_by_role(value, orders, step):
    members, blocks = lax.axis_size("dp"), lax.axis_size("space")
    pairs = []
    for member in range(members):
        for block in range(blocks):
            axis, bit = orders[member % 2][step]
            target = (member ^ bit, block) if axis == "dp" else (member, block ^ bit)
            pairs.append((member * blocks + block, target[0] * blocks + target[1]))
    return lax.ppermute(value, ("dp", "space"), pairs)


def kept(part):
    return part[: part.shape[0] // 2]


def sent(part):
    return part[part.shape[0] // 2 :].astype(F16)


def add(part, back):
    return part.astype(F32) + back.astype(F32)


def shards(features, grad_out, weight, alive):
    _, rows, columns, in_channels = features.shape
    out_channels = grad_out.shape[-1]
    pixels = rows * columns
    member_count = lax.axis_size("dp")
    core = ("dp", 1)
    across = [name for name in bits_of("dp") if name != core]
    along = bits_of("space")[::-1]
    first, inner, final_bit = along[:1], along[1:-1], along[-1:]
    orders = (across + first + inner + final_bit, first + inner + across + final_bit)
    centre_order = inner + across + first + final_bit

    own_alive = jnp.sum(alive).astype(F32)
    term_scale = (own_alive * (4.0 / member_count)).reshape(1)
    tile = grad_out.reshape(rows, columns, out_channels)
    image = features.reshape(pixels, in_channels)
    place = jnp.stack([lax.axis_index("dp"), lax.axis_index("space")]).astype(jnp.int32)

    def term(image, rows_of, streams, turned=True):
        *given, first, second = kernel_term(
            columns, place, term_scale, image, rows_of, streams, turned
        )
        return [*given, first.astype(F16), second.astype(F16)]

    def in_hbm(value):
        return pltpu.with_memory_space_constraint(value, pltpu.HBM)

    near, far = halo_rows(tile)
    width = 3 * out_channels
    image, *centre = term(
        in_hbm(image), [[in_hbm(flat(tile))]], [(width, [centre_order] * 2)], False
    )
    alive_all = [own_alive.reshape(1)]
    for away in range(1, member_count):
        alive_all.append(exchange(alive_all[0], "dp", away))
    near, far, centre, alive_all = lax.optimization_barrier((near, far, centre, alive_all))

    first_rows = either(near[0], far[0]), either(far[0], near[0])
    other = exchange(jnp.stack([near[1], far[1]]), *core)
    back = exchange(centre[0], *core)
    first = term(image, [after(first_rows, centre)], [(width, orders)])
    first, other, back = lax.optimization_barrier((first, other, back))
    second_rows = either(other[1], other[0]), either(other[0], other[1])
    centre = add(centre[1], back)
    back = exchange(first[0], *core)
    second = term(image, [after(second_rows, first, centre)], [(width, orders)])
    second, back = lax.optimization_barrier((second, back))
    ring = [None, add(second[1], back)]
    below = [either(*rows) for rows in zip(first_rows, second_rows)]
    above = [either(*rows) for rows in zip(second_rows, first_rows)]
    back, below, above = lax.optimization_barrier((exchange(second[0], *core), below, above))
    ring[0] = add(first[1], back)

    blocks = in_channels // CHANNELS_PER_STEP
    cuts = [0, blocks * 3 // 8, blocks * 5 // 8, blocks]
    last = len(centre_order) - 1
    rows_of = [below, [in_hbm(flat(tile))], above]
    chains = [[ring[1], orders, None], [centre, (centre_order, centre_order), None], [ring[0], orders, None]]
    grad_features = token = None

    def next_columns(turn, *operands):
        return input_grad(
            columns,
            scale,
            after(rows_of, *operands),
            weight,
            cuts[turn],
            cuts[turn + 1] - cuts[turn],
            grad_features,
        )

    for step in range(last):
        operands = []
        for chain in chains:
            part, order, back = chain
            if step:
                part = add(kept(part), after(back, token))
            token = sent(part)
            operands.append(token)
            chain[0], chain[2] = part, exchange_by_role(token, order, step)
            if step == last - 1 and chain is chains[0]:
                token = grad_features = next_columns(1, token)
        if step == 0:
            survivors = sum(after(alive_all, *operands))
            scale = own_alive / survivors
            token = grad_features = next_columns(0, *operands)
    parts = []
    for part, order, back in chains:
        parts.append(add(kept(part), after(back, token)))
        token = sent(parts[-1])
        if len(parts) == 1:
            ahead = exchange(token, *centre_order[last])
    operands = jnp.concatenate([sent(part) for part in parts[1:]], axis=-1)
    back = exchange(operands, *centre_order[last])
    grad_features = next_columns(2, operands)
    back, ahead, grad_features = lax.optimization_barrier((back, ahead, grad_features))
    second, centre, first = (
        add(kept(part), value)[0]
        for part, value in zip(parts, (ahead, back[..., :width], back[..., width:]))
    )
    final = jnp.concatenate([either(first, second), centre, either(second, first)], axis=-1)
    final = final * (member_count * 0.25 / survivors)
    return (final.reshape(-1, out_channels), grad_features.reshape(features.shape))


def solution(mesh):
    in_specs = (P("dp", "space", None, None), P("dp", "space", None, None), P(), P("dp"))
    out_specs = (P(("dp", "space"), None), P("dp", "space", None, None))
    return jax.shard_map(shards, mesh=mesh, in_specs=in_specs, out_specs=out_specs, check_vma=False)
```

```python
import functools

import jax
import jax.numpy as jnp
from jax import lax
from jax.experimental import pallas as pl
from jax.experimental.pallas import tpu as pltpu
from jax.sharding import PartitionSpec as P

KERNEL_DILATION = 18
CHANNELS_PER_STEP = 256
F32, F16, BF16 = jnp.float32, jnp.float16, jnp.bfloat16


def from_behind(value, axis, steps):
    count = lax.axis_size(axis)
    leading, last = (max(0, -steps), min(count, count - steps))
    return lax.ppermute(value, axis, [(source, source + steps) for source in range(leading, last)])


def exchange(value, axis, bit):
    return lax.ppermute(value, axis, [(i, i ^ bit) for i in range(lax.axis_size(axis))])


def either(first, second):
    return jnp.where(lax.axis_index("dp") % 2 == 0, first, second)


def halo_rows(tile):
    members, blocks = lax.axis_size("dp"), lax.axis_size("space")
    away, rest = divmod(KERNEL_DILATION, tile.shape[0])
    assert tile.shape[0] == 2 * rest

    def fetched(value, distance):
        pairs = []
        for member in range(members):
            for block in range(blocks):
                target = block + distance * (1 if member % 2 else -1)
                if 0 <= target < blocks:
                    pairs.append((member * blocks + block, member * blocks + target))
        return lax.ppermute(value, ("dp", "space"), pairs)

    tiles = (tile, exchange(tile, "dp", 1))
    near = fetched(jnp.stack([either(t[rest:], t[:rest]) for t in tiles]), away)
    far = fetched(jnp.stack([either(t[:rest], t[rest:]) for t in tiles]), away + 1)
    return near, far


def flat(piece):
    return piece.reshape(-1, piece.shape[-1])


def shift_columns(columns, pieces, out_ref, base):
    value = jnp.concatenate([ref[...].astype(F32) for ref in pieces])
    pixels, width = value.shape
    place = lax.broadcasted_iota(jnp.int32, (pixels, 128), 0).astype(F32)
    column = place - jnp.floor((place + 0.5) * (1.0 / columns)) * columns
    column = jnp.concatenate([column] * (width // 128), axis=1)
    ahead = pltpu.roll(value, pixels - KERNEL_DILATION, 0)
    behind = pltpu.roll(value, KERNEL_DILATION, 0)
    ahead = jnp.where(column < columns - KERNEL_DILATION, ahead, 0.0)
    behind = jnp.where(column >= KERNEL_DILATION, behind, 0.0)
    out_ref[:, base : base + width] = ahead.astype(BF16)
    out_ref[:, base + width : base + 2 * width] = value.astype(BF16)
    out_ref[:, base + 2 * width : base + 3 * width] = behind.astype(BF16)


def shift_rows(columns, cuts, pieces, out_ref):
    at = 0
    for row, cut in enumerate(cuts):
        width = pieces[at].shape[1]
        shift_columns(columns, pieces[at : at + cut], out_ref, 3 * row * width)
        at += cut


def place_in(order, member, block):
    spot = 0
    for axis, bit in order:
        spot = 2 * spot + ((member if axis == "dp" else block) // bit) % 2
    return spot


def kernel_term_kernel(columns, cuts, streams, parts, turned, place_ref, scale_ref, *refs):
    count = 1 if turned else parts
    images, pieces, outs, shifted_ref = refs[:count], refs[count:-3], refs[-3:-1], refs[-1]
    if not turned:
        pieces, turned_ref = pieces[:-1], pieces[-1]

    @pl.when(pl.program_id(0) == 0)
    def _():
        shift_rows(columns, cuts, pieces, shifted_ref)

    blocks = lax.axis_size("space")

    def products(side, out_ref):
        channels = out_ref.shape[1]
        for i in range(parts):
            if turned:
                image = images[0][0, i]
            else:
                image = images[i][...].T
                turned_ref[0, i] = image
            product = jnp.dot(image, shifted_ref[...], preferred_element_type=F32)
            product = product * scale_ref[0]
            for j in range(blocks):
                block = jnp.bitwise_xor(j, place_ref[1])
                rows = product[j * channels : (j + 1) * channels]
                at = 0
                for width, orders in streams:
                    spots = [place_in(order, 2 * i, block) for order in orders]
                    spot = jnp.where(place_ref[0] % 2 == side, spots[1], spots[0])
                    out_ref[spot, :, at : at + width] = rows[:, at : at + width]
                    at += width

    for side, out_ref in enumerate(outs):

        @pl.when(pl.program_id(0) == side)
        def _():
            products(side, out_ref)


def kernel_term(columns, place, scale, image, rows_of, streams, turned):
    channels = image.size // image.shape[-1] if turned else image.shape[1]
    pixels = image.shape[-1] if turned else image.shape[0]
    members, blocks = lax.axis_size("dp"), lax.axis_size("space")
    step, half = channels // members, members // 2
    pieces = [flat(piece) for row in rows_of for piece in row]
    cuts = tuple(len(row) for row in rows_of)
    width = 3 * len(cuts) * pieces[0].shape[1]

    def segment(i):
        return pl.BlockSpec(
            (pixels, step), lambda side, place: (0, jnp.bitwise_xor(2 * i + 1 - side, place[0]))
        )

    shapes = [(half * blocks, step // blocks, width)] * 2
    turned_block = pl.BlockSpec((1, half, step, pixels), lambda side, place: (side, 0, 0, 0))
    turned_shape = jax.ShapeDtypeStruct((2, half, step, pixels), BF16)
    return pl.pallas_call(
        functools.partial(kernel_term_kernel, columns, cuts, streams, half, turned),
        grid_spec=pltpu.PrefetchScalarGridSpec(
            num_scalar_prefetch=1,
            grid=(2,),
            in_specs=[
                pl.BlockSpec(memory_space=pltpu.SMEM),
                *([turned_block] if turned else [segment(i) for i in range(half)]),
                *[pl.BlockSpec(piece.shape, lambda side, place: (0, 0)) for piece in pieces],
            ],
            out_specs=([] if turned else [turned_block])
            + [pl.BlockSpec(shape, lambda side, place: (0, 0, 0)) for shape in shapes],
            scratch_shapes=[pltpu.VMEM((pixels, width), BF16)],
        ),
        out_shape=([] if turned else [turned_shape])
        + [jax.ShapeDtypeStruct(shape, F32) for shape in shapes],
        compiler_params=pltpu.CompilerParams(vmem_limit_bytes=26 << 20),
        cost_estimate=pl.CostEstimate(
            flops=2 * pixels * channels * width,
            bytes_accessed=2 * pixels * channels + 4 * channels * width,
            transcendentals=0,
        ),
        name="kernel_term",
    )(place, scale, *[image] * (1 if turned else half), *pieces)


def input_grad_kernel(columns, cuts, scale_ref, *refs):
    pieces = refs[: sum(cuts) or 1]
    weight_ref = refs[len(pieces)]
    wide_ref, taps_ref = refs[-2:]
    out_ref, shifted_ref = refs[-4:-2] if cuts else (refs[-3], pieces[0])
    step = out_ref.shape[1]
    width = weight_ref.shape[1]
    halves = width // 128

    if cuts:

        @pl.when(pl.program_id(0) == 0)
        def _():
            shift_rows(columns, cuts, pieces, shifted_ref)

    for h in range(halves):
        wide_ref[h] = weight_ref[:, h * 128 : (h + 1) * 128].astype(F32)
    for t in range(9):
        for h in range(halves):
            base = t * width + h * 128
            taps_ref[:, base : base + 128] = wide_ref[h, pl.ds(t, step, stride=9), :].astype(BF16)
    total = lax.dot_general(
        shifted_ref[...], taps_ref[...], (((1,), (1,)), ((), ())), preferred_element_type=F32
    )
    out_ref[...] = (total * scale_ref[0]).astype(BF16)


def input_grad(columns, scale, rows_of, weight, first, count, before=None):
    reuse = before is not None
    pieces = [rows_of] if reuse else [flat(piece) for row in rows_of for piece in row]
    cuts = () if reuse else tuple(len(row) for row in rows_of)
    pixels = pieces[0].shape[0] if reuse else sum(piece.shape[0] for piece in pieces) // 3
    rows, width = weight.shape
    channels = rows // 9
    step = CHANNELS_PER_STEP
    results = [
        (
            pl.BlockSpec((pixels, step), lambda i: (0, i + first)),
            jax.ShapeDtypeStruct((pixels, channels), BF16),
        )
    ]
    if not reuse:
        shape = (pixels, 9 * width)
        results.append((pl.BlockSpec(shape, lambda i: (0, 0)), jax.ShapeDtypeStruct(shape, BF16)))
    parts = pl.pallas_call(
        functools.partial(input_grad_kernel, columns, cuts),
        grid=(count,),
        in_specs=[
            pl.BlockSpec(memory_space=pltpu.SMEM),
            *[pl.BlockSpec(piece.shape, lambda i: (0, 0)) for piece in pieces],
            pl.BlockSpec((9 * step, width), lambda i: (i + first, 0)),
            *[pl.BlockSpec(memory_space=pl.ANY) for _ in range(reuse)],
        ],
        out_specs=[spec for spec, _ in results],
        out_shape=[kind for _, kind in results],
        input_output_aliases={len(pieces) + 2: 0} if reuse else {},
        scratch_shapes=[
            pltpu.VMEM((width // 128, 9 * step, 128), F32),
            pltpu.VMEM((step, 9 * width), BF16),
        ],
        compiler_params=pltpu.CompilerParams(vmem_limit_bytes=26 << 20),
        cost_estimate=pl.CostEstimate(
            flops=2 * pixels * 9 * width * step * count,
            bytes_accessed=2 * (9 * step * width + pixels * step) * count,
            transcendentals=0,
        ),
        name="input_grad",
    )(
        scale,
        *pieces,
        pltpu.with_memory_space_constraint(weight, pltpu.HBM),
        *([before] if reuse else []),
    )
    return (parts[0], rows_of) if reuse else tuple(parts)


def bits_of(axis):
    return [(axis, 1 << k) for k in reversed(range(lax.axis_size(axis).bit_length() - 1))]


def after(value, *others):
    return lax.optimization_barrier((value, others))[0]


def exchange_by_role(value, orders, step):
    members, blocks = lax.axis_size("dp"), lax.axis_size("space")
    pairs = []
    for member in range(members):
        for block in range(blocks):
            axis, bit = orders[member % 2][step]
            target = (member ^ bit, block) if axis == "dp" else (member, block ^ bit)
            pairs.append((member * blocks + block, target[0] * blocks + target[1]))
    return lax.ppermute(value, ("dp", "space"), pairs)


def kept(part):
    return part[: part.shape[0] // 2]


def sent(part):
    return part[part.shape[0] // 2 :].astype(F16)


def add(part, back):
    return part.astype(F32) + back.astype(F32)


def shards(features, grad_out, weight, alive):
    _, rows, columns, in_channels = features.shape
    out_channels = grad_out.shape[-1]
    pixels = rows * columns
    member_count = lax.axis_size("dp")
    core = ("dp", 1)
    across = [name for name in bits_of("dp") if name != core]
    along = bits_of("space")[::-1]
    first, inner, final_bit = along[:1], along[1:-1], along[-1:]
    orders = (across + first + inner + final_bit, first + inner + across + final_bit)
    centre_order = inner + across + first + final_bit

    own_alive = jnp.sum(alive).astype(F32)
    term_scale = (own_alive * (4.0 / member_count)).reshape(1)
    tile = grad_out.reshape(rows, columns, out_channels)
    image = features.reshape(pixels, in_channels)
    place = jnp.stack([lax.axis_index("dp"), lax.axis_index("space")]).astype(jnp.int32)

    def term(image, rows_of, streams, turned=True):
        *given, first, second = kernel_term(
            columns, place, term_scale, image, rows_of, streams, turned
        )
        return [*given, first.astype(F16), second.astype(F16)]

    def in_hbm(value):
        return pltpu.with_memory_space_constraint(value, pltpu.HBM)

    near, far = halo_rows(tile)
    width = 3 * out_channels
    image, *centre = term(
        in_hbm(image), [[in_hbm(flat(tile))]], [(width, [centre_order] * 2)], False
    )
    pair = own_alive.reshape(1)
    pair = pair + exchange(pair, *core)
    near, far, centre, pair = lax.optimization_barrier((near, far, centre, pair))
    alive_all = [pair]
    for away in range(2, member_count, 2):
        alive_all.append(exchange(pair, "dp", away))

    first_rows = either(near[0], far[0]), either(far[0], near[0])
    other = exchange(jnp.stack([near[1], far[1]]), *core)
    back = exchange(centre[0], *core)
    first = term(image, [after(first_rows, centre)], [(width, orders)])
    first, other, back, alive_all = lax.optimization_barrier((first, other, back, alive_all))
    second_rows = either(other[1], other[0]), either(other[0], other[1])
    centre = add(centre[1], back)
    back = exchange(first[0], *core)
    second = term(image, [after(second_rows, first, centre)], [(width, orders)])
    second, back = lax.optimization_barrier((second, back))
    ring = [None, add(second[1], back)]
    below = [either(*rows) for rows in zip(first_rows, second_rows)]
    above = [either(*rows) for rows in zip(second_rows, first_rows)]
    back, below, above = lax.optimization_barrier((exchange(second[0], *core), below, above))
    ring[0] = add(first[1], back)

    blocks = in_channels // CHANNELS_PER_STEP
    cuts = [0, blocks * 2 // 8, blocks * 5 // 8, blocks]
    last = len(centre_order) - 1
    rows_of = [below, [in_hbm(flat(tile))], above]
    chains = [[ring[1], orders, None], [centre, (centre_order, centre_order), None], [ring[0], orders, None]]
    grad_features = token = None

    def next_columns(turn, rows_of, *operands):
        return input_grad(
            columns,
            scale,
            after(rows_of, *operands),
            weight,
            cuts[turn],
            cuts[turn + 1] - cuts[turn],
            grad_features,
        )

    for step in range(last):
        operands = []
        for chain in chains:
            part, order, back = chain
            if step:
                part = add(kept(part), after(back, token))
            token = sent(part)
            operands.append(token)
            chain[0], chain[2] = part, exchange_by_role(token, order, step)
            if step == last - 1 and chain is chains[0]:
                grad_features, rows_of = next_columns(1, rows_of, token)
                token = grad_features
        if step == 0:
            survivors = sum(after(alive_all, *operands))
            scale = own_alive / survivors
            grad_features, rows_of = next_columns(0, rows_of, *operands)
            token = grad_features
    parts = []
    for part, order, back in chains:
        parts.append(add(kept(part), after(back, token)))
        token = sent(parts[-1])
        if len(parts) == 1:
            ahead = exchange(token, *centre_order[last])
    operands = jnp.concatenate([sent(part) for part in parts[1:]], axis=-1)
    back = exchange(operands, *centre_order[last])
    grad_features, _ = next_columns(2, rows_of, operands)
    back, ahead, grad_features = lax.optimization_barrier((back, ahead, grad_features))
    second, centre, first = (
        add(kept(part), value)[0]
        for part, value in zip(parts, (ahead, back[..., :width], back[..., width:]))
    )
    final = jnp.concatenate([either(first, second), centre, either(second, first)], axis=-1)
    final = final * (member_count * 0.25 / survivors)
    return (final.reshape(-1, out_channels), grad_features.reshape(features.shape))


def solution(mesh):
    in_specs = (P("dp", "space", None, None), P("dp", "space", None, None), P(), P("dp"))
    out_specs = (P(("dp", "space"), None), P("dp", "space", None, None))
    return jax.shard_map(shards, mesh=mesh, in_specs=in_specs, out_specs=out_specs, check_vma=False)
```

```python
import functools

import jax
import jax.numpy as jnp
from jax import lax
from jax.experimental import pallas as pl
from jax.experimental.pallas import tpu as pltpu
from jax.sharding import PartitionSpec as P

KERNEL_DILATION = 18
CHANNELS_PER_STEP = 512
F32, F16, BF16 = jnp.float32, jnp.float16, jnp.bfloat16


def from_behind(value, axis, steps):
    count = lax.axis_size(axis)
    leading, last = (max(0, -steps), min(count, count - steps))
    return lax.ppermute(value, axis, [(source, source + steps) for source in range(leading, last)])


def exchange(value, axis, bit):
    return lax.ppermute(value, axis, [(i, i ^ bit) for i in range(lax.axis_size(axis))])


def either(first, second):
    return jnp.where(lax.axis_index("dp") % 2 == 0, first, second)


def halo_rows(tile):
    members, blocks = lax.axis_size("dp"), lax.axis_size("space")
    away, rest = divmod(KERNEL_DILATION, tile.shape[0])
    assert tile.shape[0] == 2 * rest

    def fetched(value, distance):
        pairs = []
        for member in range(members):
            for block in range(blocks):
                target = block + distance * (1 if member % 2 else -1)
                if 0 <= target < blocks:
                    pairs.append((member * blocks + block, member * blocks + target))
        return lax.ppermute(value, ("dp", "space"), pairs)

    tiles = (tile, exchange(tile, "dp", 1))
    near = fetched(jnp.stack([either(t[rest:], t[:rest]) for t in tiles]), away)
    far = fetched(jnp.stack([either(t[:rest], t[rest:]) for t in tiles]), away + 1)
    return near, far


def flat(piece):
    return piece.reshape(-1, piece.shape[-1])


def shift_columns(columns, pieces, out_ref, base):
    value = jnp.concatenate([ref[...].astype(F32) for ref in pieces])
    pixels, width = value.shape
    place = lax.broadcasted_iota(jnp.int32, (pixels, 128), 0).astype(F32)
    column = place - jnp.floor((place + 0.5) * (1.0 / columns)) * columns
    column = jnp.concatenate([column] * (width // 128), axis=1)
    ahead = pltpu.roll(value, pixels - KERNEL_DILATION, 0)
    behind = pltpu.roll(value, KERNEL_DILATION, 0)
    ahead = jnp.where(column < columns - KERNEL_DILATION, ahead, 0.0)
    behind = jnp.where(column >= KERNEL_DILATION, behind, 0.0)
    out_ref[:, base : base + width] = ahead.astype(BF16)
    out_ref[:, base + width : base + 2 * width] = value.astype(BF16)
    out_ref[:, base + 2 * width : base + 3 * width] = behind.astype(BF16)


def shift_rows(columns, cuts, pieces, out_ref):
    at = 0
    for row, cut in enumerate(cuts):
        width = pieces[at].shape[1]
        shift_columns(columns, pieces[at : at + cut], out_ref, 3 * row * width)
        at += cut


def place_in(order, member, block):
    spot = 0
    for axis, bit in order:
        spot = 2 * spot + ((member if axis == "dp" else block) // bit) % 2
    return spot


def kernel_term_kernel(columns, cuts, streams, parts, turned, place_ref, scale_ref, *refs):
    count = 1 if turned else parts
    images, pieces, outs, shifted_ref = refs[:count], refs[count:-3], refs[-3:-1], refs[-1]
    if not turned:
        pieces, turned_ref = pieces[:-1], pieces[-1]

    @pl.when(pl.program_id(0) == 0)
    def _():
        shift_rows(columns, cuts, pieces, shifted_ref)

    blocks = lax.axis_size("space")

    def products(side, out_ref):
        channels = out_ref.shape[1]
        for i in range(parts):
            if turned:
                image = images[0][0, i]
            else:
                image = images[i][...].T
                turned_ref[0, i] = image
            product = jnp.dot(image, shifted_ref[...], preferred_element_type=F32)
            product = product * scale_ref[0]
            for j in range(blocks):
                block = jnp.bitwise_xor(j, place_ref[1])
                rows = product[j * channels : (j + 1) * channels]
                at = 0
                for width, orders in streams:
                    spots = [place_in(order, 2 * i, block) for order in orders]
                    spot = jnp.where(place_ref[0] % 2 == side, spots[1], spots[0])
                    out_ref[spot, :, at : at + width] = rows[:, at : at + width]
                    at += width

    for side, out_ref in enumerate(outs):

        @pl.when(pl.program_id(0) == side)
        def _():
            products(side, out_ref)


def kernel_term(columns, place, scale, image, rows_of, streams, turned):
    channels = image.size // image.shape[-1] if turned else image.shape[1]
    pixels = image.shape[-1] if turned else image.shape[0]
    members, blocks = lax.axis_size("dp"), lax.axis_size("space")
    step, half = channels // members, members // 2
    pieces = [flat(piece) for row in rows_of for piece in row]
    cuts = tuple(len(row) for row in rows_of)
    width = 3 * len(cuts) * pieces[0].shape[1]

    def segment(i):
        return pl.BlockSpec(
            (pixels, step), lambda side, place: (0, jnp.bitwise_xor(2 * i + 1 - side, place[0]))
        )

    shapes = [(half * blocks, step // blocks, width)] * 2
    turned_block = pl.BlockSpec((1, half, step, pixels), lambda side, place: (side, 0, 0, 0))
    turned_shape = jax.ShapeDtypeStruct((2, half, step, pixels), BF16)
    return pl.pallas_call(
        functools.partial(kernel_term_kernel, columns, cuts, streams, half, turned),
        grid_spec=pltpu.PrefetchScalarGridSpec(
            num_scalar_prefetch=1,
            grid=(2,),
            in_specs=[
                pl.BlockSpec(memory_space=pltpu.SMEM),
                *([turned_block] if turned else [segment(i) for i in range(half)]),
                *[pl.BlockSpec(piece.shape, lambda side, place: (0, 0)) for piece in pieces],
            ],
            out_specs=([] if turned else [turned_block])
            + [pl.BlockSpec(shape, lambda side, place: (0, 0, 0)) for shape in shapes],
            scratch_shapes=[pltpu.VMEM((pixels, width), BF16)],
        ),
        out_shape=([] if turned else [turned_shape])
        + [jax.ShapeDtypeStruct(shape, F32) for shape in shapes],
        compiler_params=pltpu.CompilerParams(vmem_limit_bytes=32 << 20),
        cost_estimate=pl.CostEstimate(
            flops=2 * pixels * channels * width,
            bytes_accessed=2 * pixels * channels + 4 * channels * width,
            transcendentals=0,
        ),
        name="kernel_term",
    )(place, scale, *[image] * (1 if turned else half), *pieces)


def input_grad_kernel(columns, cuts, scale_ref, *refs):
    pieces = refs[: sum(cuts) or 1]
    weight_ref = refs[len(pieces)]
    wide_ref, taps_ref = refs[-2:]
    out_ref, shifted_ref = refs[-4:-2] if cuts else (refs[-3], pieces[0])
    step = out_ref.shape[1]
    width = weight_ref.shape[1]
    halves = width // 128

    if cuts:

        @pl.when(pl.program_id(0) == 0)
        def _():
            shift_rows(columns, cuts, pieces, shifted_ref)

    for h in range(halves):
        wide_ref[h] = weight_ref[:, h * 128 : (h + 1) * 128].astype(F32)
    for t in range(9):
        for h in range(halves):
            base = t * width + h * 128
            taps_ref[:, base : base + 128] = wide_ref[h, pl.ds(t, step, stride=9), :].astype(BF16)
    total = lax.dot_general(
        shifted_ref[...], taps_ref[...], (((1,), (1,)), ((), ())), preferred_element_type=F32
    )
    out_ref[...] = (total * scale_ref[0]).astype(BF16)


def input_grad(columns, scale, rows_of, weight, first, count, before=None):
    reuse = before is not None
    pieces = [rows_of] if reuse else [flat(piece) for row in rows_of for piece in row]
    cuts = () if reuse else tuple(len(row) for row in rows_of)
    pixels = pieces[0].shape[0] if reuse else sum(piece.shape[0] for piece in pieces) // 3
    rows, width = weight.shape
    channels = rows // 9
    step = CHANNELS_PER_STEP
    results = [
        (
            pl.BlockSpec((pixels, step), lambda i: (0, i + first)),
            jax.ShapeDtypeStruct((pixels, channels), BF16),
        )
    ]
    if not reuse:
        shape = (pixels, 9 * width)
        results.append((pl.BlockSpec(shape, lambda i: (0, 0)), jax.ShapeDtypeStruct(shape, BF16)))
    parts = pl.pallas_call(
        functools.partial(input_grad_kernel, columns, cuts),
        grid=(count,),
        in_specs=[
            pl.BlockSpec(memory_space=pltpu.SMEM),
            *[pl.BlockSpec(piece.shape, lambda i: (0, 0)) for piece in pieces],
            pl.BlockSpec((9 * step, width), lambda i: (i + first, 0)),
            *[pl.BlockSpec(memory_space=pl.ANY) for _ in range(reuse)],
        ],
        out_specs=[spec for spec, _ in results],
        out_shape=[kind for _, kind in results],
        input_output_aliases={len(pieces) + 2: 0} if reuse else {},
        scratch_shapes=[
            pltpu.VMEM((width // 128, 9 * step, 128), F32),
            pltpu.VMEM((step, 9 * width), BF16),
        ],
        compiler_params=pltpu.CompilerParams(vmem_limit_bytes=32 << 20),
        cost_estimate=pl.CostEstimate(
            flops=2 * pixels * 9 * width * step * count,
            bytes_accessed=2 * (9 * step * width + pixels * step) * count,
            transcendentals=0,
        ),
        name="input_grad",
    )(
        scale,
        *pieces,
        pltpu.with_memory_space_constraint(weight, pltpu.HBM),
        *([before] if reuse else []),
    )
    return (parts[0], rows_of) if reuse else tuple(parts)


def bits_of(axis):
    return [(axis, 1 << k) for k in reversed(range(lax.axis_size(axis).bit_length() - 1))]


def after(value, *others):
    return lax.optimization_barrier((value, others))[0]


def exchange_by_role(value, orders, step):
    members, blocks = lax.axis_size("dp"), lax.axis_size("space")
    pairs = []
    for member in range(members):
        for block in range(blocks):
            axis, bit = orders[member % 2][step]
            target = (member ^ bit, block) if axis == "dp" else (member, block ^ bit)
            pairs.append((member * blocks + block, target[0] * blocks + target[1]))
    return lax.ppermute(value, ("dp", "space"), pairs)


def kept(part):
    return part[: part.shape[0] // 2]


def sent(part):
    return part[part.shape[0] // 2 :].astype(F16)


def add(part, back):
    return part.astype(F32) + back.astype(F32)


def shards(features, grad_out, weight, alive):
    _, rows, columns, in_channels = features.shape
    out_channels = grad_out.shape[-1]
    pixels = rows * columns
    member_count = lax.axis_size("dp")
    core = ("dp", 1)
    across = [name for name in bits_of("dp") if name != core]
    along = bits_of("space")[::-1]
    first, inner, final_bit = along[:1], along[1:-1], along[-1:]
    orders = (across + first + inner + final_bit, first + inner + across + final_bit)
    centre_order = inner + across + first + final_bit

    own_alive = jnp.sum(alive).astype(F32)
    term_scale = (own_alive * (4.0 / member_count)).reshape(1)
    tile = grad_out.reshape(rows, columns, out_channels)
    image = features.reshape(pixels, in_channels)
    place = jnp.stack([lax.axis_index("dp"), lax.axis_index("space")]).astype(jnp.int32)

    def term(image, rows_of, streams, turned=True):
        *given, first, second = kernel_term(
            columns, place, term_scale, image, rows_of, streams, turned
        )
        return [*given, first.astype(F16), second.astype(F16)]

    def in_hbm(value):
        return pltpu.with_memory_space_constraint(value, pltpu.HBM)

    near, far = halo_rows(tile)
    width = 3 * out_channels
    image, *centre = term(
        in_hbm(image), [[in_hbm(flat(tile))]], [(width, [centre_order] * 2)], False
    )
    pair = own_alive.reshape(1)
    pair = pair + exchange(pair, *core)
    near, far, centre, pair = lax.optimization_barrier((near, far, centre, pair))
    alive_all = [pair]
    for away in range(2, member_count, 2):
        alive_all.append(exchange(pair, "dp", away))

    first_rows = either(near[0], far[0]), either(far[0], near[0])
    other = exchange(jnp.stack([near[1], far[1]]), *core)
    back = exchange(centre[0], *core)
    first = term(image, [after(first_rows, centre)], [(width, orders)])
    first, other, back, alive_all = lax.optimization_barrier((first, other, back, alive_all))
    second_rows = either(other[1], other[0]), either(other[0], other[1])
    centre = add(centre[1], back)
    back = exchange(first[0], *core)
    second = term(image, [after(second_rows, first, centre)], [(width, orders)])
    second, back = lax.optimization_barrier((second, back))
    ring = [None, add(second[1], back)]
    below = [either(*rows) for rows in zip(first_rows, second_rows)]
    above = [either(*rows) for rows in zip(second_rows, first_rows)]
    back, below, above = lax.optimization_barrier((exchange(second[0], *core), below, above))
    ring[0] = add(first[1], back)

    blocks = in_channels // CHANNELS_PER_STEP
    cuts = [0, blocks * 2 // 8, blocks * 5 // 8, blocks]
    last = len(centre_order) - 1
    rows_of = [below, [in_hbm(flat(tile))], above]
    chains = [[ring[1], orders, None], [centre, (centre_order, centre_order), None], [ring[0], orders, None]]
    grad_features = token = None

    def next_columns(turn, rows_of, *operands):
        return input_grad(
            columns,
            scale,
            after(rows_of, *operands),
            weight,
            cuts[turn],
            cuts[turn + 1] - cuts[turn],
            grad_features,
        )

    for step in range(last):
        operands = []
        for chain in chains:
            part, order, back = chain
            if step:
                part = add(kept(part), after(back, token))
            token = sent(part)
            operands.append(token)
            chain[0], chain[2] = part, exchange_by_role(token, order, step)
            if step == last - 1 and chain is chains[0]:
                grad_features, rows_of = next_columns(1, rows_of, token)
                token = grad_features
        if step == 0:
            survivors = sum(after(alive_all, *operands))
            scale = own_alive / survivors
            grad_features, rows_of = next_columns(0, rows_of, *operands)
            token = grad_features
    parts = []
    for part, order, back in chains:
        parts.append(add(kept(part), after(back, token)))
        token = sent(parts[-1])
        if len(parts) == 1:
            ahead = exchange(token, *centre_order[last])
    operands = jnp.concatenate([sent(part) for part in parts[1:]], axis=-1)
    back = exchange(operands, *centre_order[last])
    grad_features, _ = next_columns(2, rows_of, operands)
    back, ahead, grad_features = lax.optimization_barrier((back, ahead, grad_features))
    second, centre, first = (
        add(kept(part), value)[0]
        for part, value in zip(parts, (ahead, back[..., :width], back[..., width:]))
    )
    final = jnp.concatenate([either(first, second), centre, either(second, first)], axis=-1)
    final = final * (member_count * 0.25 / survivors)
    return (final.reshape(-1, out_channels), grad_features.reshape(features.shape))


def solution(mesh):
    in_specs = (P("dp", "space", None, None), P("dp", "space", None, None), P(), P("dp"))
    out_specs = (P(("dp", "space"), None), P("dp", "space", None, None))
    return jax.shard_map(shards, mesh=mesh, in_specs=in_specs, out_specs=out_specs, check_vma=False)
```
